256 devices in a mesh: jgrp: 16 (over y, x), energy: 16 (over z, core).
Axes of the slice: x: 4, y: 4, z: 8, core: 2. Of those that a mesh axis runs over, the one named last changes fastest.
Arguments:
- s_real: bfloat16 [32, 256, 256, 256], P('jgrp', 'energy'), may hold values from -3 to 3
- s_imag: bfloat16 [32, 256, 256, 256], P('jgrp', 'energy'), may hold values from -3 to 3
- level_map: int32 [32, 256], P('jgrp'), may hold values from 0 to 511
- channel_count: int32 [32], P('jgrp'), may hold values from 1 to 256, as said below
- prefactor: float32 [512, 256], P(None, 'energy'), may hold values from 0.003 to 0.03
- maxwell: float32 [8, 256], P(None, 'energy'), may hold values from 0.000390625 to 0.00390625
Outputs:
- rates: float32 [512, 8, 512], P(('jgrp', 'energy'))
The draws below stay inside these ranges and needn't reach their ends.
Inputs may be any that keep to these rules, and one draw needn't show every extreme that they name: `channel_count`: rises with J from about 256 / 4; the last block has exactly 256.
All inputs are finite; a program needn't handle non-finite values.
Results may differ from the reference program's by a relative error of at most 0.0003.
Values sent between devices are 32-bit elements; how exact they have to be, the bound alone decides.
No kernel may reach another device: no remote copies, remote signals or barrier semaphores. Data moves between devices by JAX's collectives and lax.ppermute only.
A program may use at most 128 MiB of HBM per device.

```python
import math
import jax
import jax.numpy as jnp
from jax import lax

LEVELS = 512
CHANS = 256
NT = 8
NJ = 32
NE = 256


def draw_channel_count(key, part):
    key = jax.random.fold_in(key, 11)
    jindex = jnp.arange(NJ, dtype=jnp.int32)
    base = CHANS // 4 + jindex * (CHANS - CHANS // 4) // max(NJ - 1, 1)
    jitter = jax.random.randint(key, (NJ,), 0, CHANS // 8 + 1, dtype=jnp.int32)
    counts = jnp.clip(base - jitter, 1, CHANS)
    return jnp.where(jindex == NJ - 1, CHANS, counts).astype(jnp.int32)


def touch_ends(entries, key, low, top_value):
    longest = entries.shape.index(max(entries.shape))
    spots = []
    for shift in (0, 1):
        where = [jax.random.randint(jax.random.fold_in(key, axis), (), 0, length) for axis, length in enumerate(entries.shape)]
        where[longest] = (where[longest] + shift) % entries.shape[longest]
        spots.append(tuple(where))
    return entries.at[spots[0]].set(low).at[spots[1]].set(top_value)


def steps_of(own_key, extent, split, low, high):
    factor_of, own = 1.0, jax.random.fold_in(own_key, 6)
    for position, blocks in split:
        steps = jnp.exp(jax.random.uniform(jax.random.fold_in(own, position), (blocks,), jnp.float32, low / len(split), high / len(split)))
        factor_of = factor_of * jnp.repeat(steps, extent[position] // blocks).reshape([-1 if axis == position else 1 for axis in range(len(extent))])
    return factor_of


def normal_values(rng, extent, scale, reach, split=(), kind=jnp.bfloat16):
    array = jax.random.normal(rng, extent, jnp.float32) * scale
    if len(split) > 0:
        array = steps_of(rng, extent, split, -0.22, 0.18) * array
    return jnp.clip(array, min=-reach, max=reach).astype(kind)


def setup_inputs(seed: int = 0) -> dict:
    key_list = jax.random.split(jax.random.key(seed), 7)
    s_real = normal_values(key_list[0], (NJ, NE, CHANS, CHANS), 0.5, 3.0, ((0, 16), (1, 16)))
    s_imag = normal_values(key_list[1], (NJ, NE, CHANS, CHANS), 0.5, 3.0, ((0, 16), (1, 16)))
    level_map = touch_ends(jax.random.randint(key_list[2], (NJ, CHANS), 0, LEVELS), jax.random.fold_in(key_list[2], 1), 0, LEVELS - 1).astype(jnp.int32)
    channel_count = draw_channel_count(jax.random.fold_in(key_list[6], 71), 0)
    prefactor = jnp.clip(jnp.exp(math.log(0.03) - 2.3025851 * jax.random.uniform(key_list[4], (LEVELS, NE), jnp.float32) ** steps_of(key_list[4], (LEVELS, NE), ((1, 16),), -0.2, 0.2)), 0.003, 0.03)
    maxwell = jnp.clip(jnp.exp(math.log(0.00390625) - 2.3025851 * jax.random.uniform(key_list[5], (NT, NE), jnp.float32) ** steps_of(key_list[5], (NT, NE), ((1, 16),), -0.2, 0.2)), 0.000390625, 0.00390625)
    return dict(s_real=s_real, s_imag=s_imag, level_map=level_map, channel_count=channel_count, prefactor=prefactor, maxwell=maxwell)


def reference(s_real, s_imag, level_map, channel_count, prefactor, maxwell):
    chan = jnp.arange(CHANS, dtype=jnp.int32)
    eye = (chan[:, None] == chan[None, :]).astype(jnp.float32)

    def one_block(total, jindex):
        real_part = s_real[jindex].astype(jnp.float32)
        imag_part = s_imag[jindex].astype(jnp.float32)
        factor = (2 * jindex + 1).astype(jnp.float32)
        weighted = (((eye - real_part) ** 2 + imag_part ** 2) * factor).astype(jnp.bfloat16)
        weighted = lax.optimization_barrier(weighted).astype(jnp.float32)
        segment = jnp.where(chan < channel_count[jindex], level_map[jindex], LEVELS).astype(jnp.int32)
        rowsum = jax.ops.segment_sum(jnp.transpose(weighted, (1, 0, 2)), segment, num_segments=LEVELS + 1)[:LEVELS]
        rowsum = lax.optimization_barrier(rowsum.astype(jnp.bfloat16)).astype(jnp.float32)
        tile = jax.ops.segment_sum(jnp.transpose(rowsum, (2, 1, 0)), segment, num_segments=LEVELS + 1)[:LEVELS]
        return total + tile, None

    start = jnp.zeros((LEVELS, NE, LEVELS), jnp.float32)
    cross, _ = lax.scan(one_block, start, jnp.arange(NJ, dtype=jnp.int32))
    return jnp.einsum("fei,te,ie->itf", cross, maxwell, prefactor, precision=lax.Precision.HIGHEST)
```

```python
import functools

import jax
import jax.numpy as jnp
from jax import lax
from jax.experimental import pallas as pl
from jax.experimental.pallas import tpu as pltpu
from jax.sharding import Mesh, PartitionSpec as P

STEP = 4
GROUP = 16
HIGHEST = lax.Precision.HIGHEST


def split2(x):
    hi = x.astype(jnp.bfloat16)
    lo = (x - hi.astype(jnp.float32)).astype(jnp.bfloat16)
    return hi, lo


def iota(shape, axis):
    return lax.broadcasted_iota(jnp.int32, shape, axis)


def share_kernel(block, count_ref, level_ref, real_ref, imag_ref, pre_ref, max_ref,
                 send_ref, keep_ref, rows_ref, same_ref, scale_ref, weight_ref):
    temps, energies = max_ref.shape
    levels = pre_ref.shape[0]
    chans = real_ref.shape[-1]
    width = energies * GROUP
    step = pl.program_id(0)
    core = lax.axis_index("core")
    jgrp = lax.axis_index("y") * lax.axis_size("x") + lax.axis_index("x")
    factor = (2 * (jgrp * level_ref.shape[0] + block) + 1).astype(jnp.float32)
    eye = iota((chans, chans), 0) == iota((chans, chans), 1)

    @pl.when(step == 0)
    def _():
        lane = iota((1, chans), 1)
        seg_row = jnp.where(lane < count_ref[block], level_ref[pl.ds(block, 1), :], -1)
        seg_col = jnp.sum(
            jnp.where(eye, seg_row.astype(jnp.float32), 0.0), axis=1, keepdims=True
        ).astype(jnp.int32)
        same = (seg_col == seg_row) & (seg_col >= 0)
        earlier = same & (iota((chans, chans), 1) < iota((chans, chans), 0))
        taken = jnp.max(jnp.where(earlier, 1.0, 0.0), axis=1, keepdims=True)
        same_ref[...] = jnp.where(same & (taken == 0.0), 1.0, 0.0).astype(jnp.bfloat16)
        picks = jnp.where(seg_col == iota((chans, levels), 1), 1.0, 0.0)
        spread = jnp.where(iota((energies, width), 1) // GROUP == iota((energies, width), 0), 1.0, 0.0)
        own = jnp.dot(picks, pre_ref[...], precision=HIGHEST, preferred_element_type=jnp.float32)
        scale_ref[...] = jnp.dot(own, spread, precision=HIGHEST, preferred_element_type=jnp.float32)
        wide = jnp.dot(max_ref[...], spread, precision=HIGHEST, preferred_element_type=jnp.float32)
        hit = iota((GROUP, width), 1) % GROUP == iota((GROUP, width), 0)
        for t in range(temps):
            weight_ref[t * GROUP:(t + 1) * GROUP, :] = jnp.where(hit, wide[t:t + 1, :], 0.0)

    delta = jnp.where(eye, 1.0, 0.0)
    for e in range(STEP):
        real = real_ref[0, e].astype(jnp.float32)
        imag = imag_ref[0, e].astype(jnp.float32)
        weighted = (((delta - real) ** 2 + imag ** 2) * factor).astype(jnp.bfloat16)
        rowsum = jnp.dot(same_ref[...], weighted, preferred_element_type=jnp.float32)
        rows_ref[step * STEP + e] = rowsum.astype(jnp.bfloat16)

    @pl.when(step == pl.num_programs(0) - 1)
    def _():
        half = chans // 2
        for out_ref, base in ((send_ref, (1 - core) * half), (keep_ref, core * half)):
            for group in range(half // GROUP):
                at = pl.ds(pl.multiple_of(base + group * GROUP, GROUP), GROUP)
                part = rows_ref[:, at, :].reshape(width, chans)
                own = scale_ref[at, :]
                mix = weight_ref[...] * jnp.concatenate([own] * temps, axis=0)
                hi, lo = split2(mix)
                both = jnp.dot(jnp.concatenate([hi, lo], axis=0), part,
                               preferred_element_type=jnp.float32)
                total = both[:temps * GROUP] + both[temps * GROUP:]
                out_ref[:, group * GROUP:(group + 1) * GROUP, :] = total.reshape(temps, GROUP, chans)


def share(block, counts, level_map, s_real, s_imag, prefactor, maxwell):
    energies, chans = s_real.shape[1], s_real.shape[2]
    temps, levels = maxwell.shape[0], prefactor.shape[0]
    width = energies * GROUP
    out = jax.ShapeDtypeStruct((temps, chans // 2, chans), jnp.float32)
    whole = pl.BlockSpec(memory_space=pltpu.VMEM)
    parts = pl.BlockSpec((1, STEP, chans, chans), lambda e: (block, e, 0, 0))
    return pl.pallas_call(
        functools.partial(share_kernel, block),
        grid=(energies // STEP,),
        out_shape=[out, out],
        in_specs=[pl.BlockSpec(memory_space=pltpu.SMEM), whole, parts, parts, whole, whole],
        out_specs=[pl.BlockSpec((temps, chans // 2, chans), lambda e: (0, 0, 0))] * 2,
        scratch_shapes=[
            pltpu.VMEM((energies, chans, chans), jnp.bfloat16),
            pltpu.VMEM((chans, chans), jnp.bfloat16),
            pltpu.VMEM((chans, width), jnp.float32),
            pltpu.VMEM((temps * GROUP, width), jnp.float32),
        ],
        compiler_params=pltpu.CompilerParams(vmem_limit_bytes=40 * 2**20),
        cost_estimate=pl.CostEstimate(flops=2 * 2 * energies * chans**3, transcendentals=0,
                                      bytes_accessed=4 * energies * chans**2 + 8 * temps * chans**2),
        name="share",
    )(counts, level_map, s_real, s_imag, prefactor, maxwell)


def spread_kernel(count_ref, level_ref, mine_ref, other_ref, out_ref):
    blocks, half, chans = mine_ref.shape
    rows, levels = out_ref.shape
    core = lax.axis_index("core")
    lane = iota((1, chans), 1)
    row = iota((rows, chans), 0)
    wanted = row // 2 * 4 + core * 2 + row % 2
    for block in range(blocks):
        seg = jnp.where(lane < count_ref[block], level_ref[pl.ds(block, 1), :], -1)
        columns = jnp.where(iota((levels, chans), 0) == seg, 1.0, 0.0).astype(jnp.bfloat16)
        picks = jnp.where(wanted == seg, 1.0, 0.0).astype(jnp.bfloat16)
        mine, other = mine_ref[block], other_ref[block]
        first = jnp.where(core == 0, mine, other)
        second = jnp.where(core == 0, other, mine)
        both = jnp.concatenate([first, second], axis=0)
        hi, lo = split2(both)
        turn = (((1,), (1,)), ((), ()))
        wide = lax.dot_general(hi, columns, turn, preferred_element_type=jnp.float32)
        wide += lax.dot_general(lo, columns, turn, preferred_element_type=jnp.float32)
        hi, lo = split2(wide)
        term = jnp.dot(picks, hi, preferred_element_type=jnp.float32)
        term += jnp.dot(picks, lo, preferred_element_type=jnp.float32)
        if block == 0:
            out_ref[...] = term
        else:
            out_ref[...] += term


def spread(counts, level_map, mine, other, levels):
    whole = pl.BlockSpec(memory_space=pltpu.VMEM)
    return pl.pallas_call(
        spread_kernel,
        out_shape=jax.ShapeDtypeStruct((levels // 2, levels), jnp.float32),
        in_specs=[pl.BlockSpec(memory_space=pltpu.SMEM), whole, whole, whole],
        out_specs=whole,
        compiler_params=pltpu.CompilerParams(vmem_limit_bytes=40 * 2**20),
        name="spread",
    )(counts, level_map, mine, other)


def ring_sum(z, n, keep, other):
    rows = keep.shape[1]
    half = rows // 2

    def own(t, low, high):
        def cut(x):
            return lax.dynamic_slice_in_dim(x, lax.rem(t + n, n), 1, 0)[0, low:high]
        return cut(keep) + cut(other)

    up = [(i, (i + 1) % n) for i in range(n)]
    down = [(i, (i - 1) % n) for i in range(n)]
    reach = n // 2
    forward = lax.ppermute(own(z + reach, 0, half), "z", up)
    backward = lax.ppermute(own(z - reach, half, rows), "z", down)
    forward = jnp.concatenate([forward + own(z + reach - 1, 0, half), own(z + reach - 1, half, rows)])
    backward = jnp.concatenate([own(z - reach + 1, 0, half), backward + own(z - reach + 1, half, rows)])
    for left in range(reach - 1, 0, -1):
        forward = lax.ppermute(forward, "z", up)
        backward = lax.ppermute(backward, "z", down)
        if left > 1:
            forward = forward + own(z + left - 1, 0, rows)
            backward = backward + own(z - left + 1, 0, rows)
    return forward + backward + own(z, 0, rows)


def body(s_real, s_imag, level_map, channel_count, prefactor, maxwell):
    blocks = s_real.shape[0]
    levels = prefactor.shape[0]
    temps = maxwell.shape[0]
    n = lax.axis_size("z")
    z = lax.axis_index("z")
    swap = [(0, 1), (1, 0)]
    sums = []
    for block in range(blocks):
        send, keep = share(block, channel_count, level_map, s_real, s_imag, prefactor, maxwell)
        other = lax.ppermute(send, "core", swap)
        sums.append(ring_sum(z, n, keep, other))
    mine = jnp.stack(sums)
    other = lax.ppermute(mine, "core", swap)
    part = spread(channel_count, level_map, mine, other, levels)
    groups = lax.axis_size("y") * lax.axis_size("x")
    part = part.reshape(groups, levels // 2 // groups, levels)
    part = lax.all_to_all(part, ("y", "x"), 0, 0, tiled=True).sum(0)
    part = lax.all_to_all(part.reshape(n, part.shape[0] // n, levels), "z", 0, 0, tiled=True)
    return jnp.transpose(part, (1, 0, 2))


def solution(mesh):
    fine = Mesh(mesh.devices.reshape(4, 4, 8, 2), ("y", "x", "z", "core"))
    jgrp, energy = ("y", "x"), ("z", "core")
    in_specs = (
        P(jgrp, energy, None, None),
        P(jgrp, energy, None, None),
        P(jgrp, None),
        P(jgrp),
        P(None, energy),
        P(None, energy),
    )
    out_specs = P(("y", "x", "z", "core"), None, None)
    return jax.shard_map(body, mesh=fine, in_specs=in_specs, out_specs=out_specs, check_vma=False)
```

```python
import functools

import jax
import jax.numpy as jnp
from jax import lax
from jax.experimental import pallas as pl
from jax.experimental.pallas import tpu as pltpu
from jax.sharding import Mesh, PartitionSpec as P

STEP = 8
GROUP = 16
LANES = 128


def split2(x):
    hi = x.astype(jnp.bfloat16)
    lo = (x - hi.astype(jnp.float32)).astype(jnp.bfloat16)
    return hi, lo


def split3(x):
    hi, mid = split2(x)
    lo = (x - hi.astype(jnp.float32) - mid.astype(jnp.float32)).astype(jnp.bfloat16)
    return hi, mid, lo


def iota(shape, axis):
    return lax.broadcasted_iota(jnp.int32, shape, axis)


def across(x, lanes):
    return jnp.concatenate([x] * (lanes // LANES), axis=1)


def share_kernel(count_hbm, level_hbm, real_hbm, imag_hbm, pre_hbm, max_hbm,
                 send_ref, keep_ref, send_rest_0, send_rest_1, keep_rest_0, keep_rest_1,
                 real_ref, imag_ref, count_ref, level_ref, pre_ref, max_ref,
                 rows_ref, same_ref, scale_ref, weight_ref, wide_ref, part_sem, small_sem):
    temps, energies = max_ref.shape
    levels = pre_ref.shape[1]
    blocks, chans = level_ref.shape
    half = chans // 2
    width = energies * GROUP
    smalls = []
    for i, pair in enumerate(((count_hbm, count_ref), (level_hbm, level_ref),
                              (pre_hbm, pre_ref), (max_hbm, max_ref))):
        smalls.append(pltpu.make_async_copy(*pair, small_sem.at[i]))
        smalls[-1].start()
    parts = []
    for block in range(blocks):
        for step in range(energies // STEP):
            at = pl.ds(step * STEP, STEP)
            parts.append([
                pltpu.make_async_copy(x_hbm.at[block, at], x_ref.at[block, at], part_sem.at[i, block, step])
                for i, (x_hbm, x_ref) in enumerate(((real_hbm, real_ref), (imag_hbm, imag_ref)))
            ])
            for copy in parts[-1]:
                copy.start()
    core = lax.axis_index("core")
    z = lax.axis_index("z")
    jgrp = lax.axis_index("y") * lax.axis_size("x") + lax.axis_index("x")
    delta = jnp.where(iota((chans, chans), 0) == iota((chans, chans), 1), 1.0, 0.0)
    turn = (((1,), (1,)), ((), ()))
    for copy in smalls:
        copy.wait()

    spread = iota((3 * energies, width), 1) // GROUP == iota((3 * energies, width), 0) % energies
    spread = jnp.where(spread, 1.0, 0.0).astype(jnp.bfloat16)
    wide_ref[...] = jnp.dot(jnp.concatenate(split3(max_ref[...]), axis=1), spread,
                            preferred_element_type=jnp.float32)
    hit = iota((GROUP, width), 1) % GROUP == iota((GROUP, width), 0)
    sign = 1 - 2 * core
    order = [z + sign * 3, z + sign * 2, z + sign, z - sign * 3, z - sign * 2, z - sign, z + 4, z]
    for s in range(temps):
        t = lax.rem(order[s] + temps, temps)
        weight_ref[s * GROUP:(s + 1) * GROUP, :] = jnp.where(hit, wide_ref[pl.ds(t, 1), :], 0.0)
    pre = jnp.concatenate(split3(pre_ref[...]), axis=0)

    for block in range(blocks):
        seg_row = jnp.where(iota((1, chans), 1) < count_ref[block], level_ref[pl.ds(block, 1), :], -1)
        seg_row = seg_row.astype(jnp.float32)
        seg_col = jnp.transpose(jnp.broadcast_to(seg_row, (LANES, chans)))
        same = across(seg_col, chans) == seg_row
        earlier = same & (iota((chans, chans), 1) < iota((chans, chans), 0))
        taken = jnp.dot(jnp.where(earlier, 1.0, 0.0).astype(jnp.bfloat16),
                        jnp.ones((chans, LANES), jnp.bfloat16), preferred_element_type=jnp.float32)
        lead = across(jnp.where((taken == 0.0) & (seg_col >= 0.0), 1.0, 0.0), chans)
        same_ref[block] = jnp.where(same, lead, 0.0).astype(jnp.bfloat16)
        picks = across(seg_col, levels) == iota((chans, levels), 1).astype(jnp.float32)
        picks = jnp.where(picks, 1.0, 0.0).astype(jnp.bfloat16)
        own = lax.dot_general(picks, pre, turn, preferred_element_type=jnp.float32)
        scale_ref[block] = jnp.dot(own.astype(jnp.bfloat16), spread, preferred_element_type=jnp.float32)

    for block in range(blocks):
        factor = (2 * (jgrp * blocks + block) + 1).astype(jnp.float32)
        for step in range(energies // STEP):
            for copy in parts[block * (energies // STEP) + step]:
                copy.wait()
            for e in range(step * STEP, (step + 1) * STEP):
                real = real_ref[block, e].astype(jnp.float32)
                imag = imag_ref[block, e].astype(jnp.float32)
                weighted = (((delta - real) ** 2 + imag ** 2) * factor).astype(jnp.bfloat16)
                rowsum = jnp.dot(same_ref[block], weighted, preferred_element_type=jnp.float32)
                rows_ref[block, e] = rowsum.astype(jnp.bfloat16)
        start = block * half
        send_rest_ref, keep_rest_ref = ((send_rest_0, keep_rest_0), (send_rest_1, keep_rest_1))[block]
        for mine in (False, True):
            base = (core if mine else 1 - core) * half
            for group in range(half // GROUP):
                at = pl.ds(pl.multiple_of(base + group * GROUP, GROUP), GROUP)
                part = rows_ref[block, :, at, :].reshape(width, chans)
                own = scale_ref[block, at, :]
                mix = weight_ref[...] * jnp.concatenate([own] * temps, axis=0)
                hi, lo = split2(mix)
                both = jnp.dot(jnp.concatenate([hi, lo], axis=0), part,
                               preferred_element_type=jnp.float32)
                total = both[:temps * GROUP] + both[temps * GROUP:]
                total = total.reshape(temps, GROUP, chans)
                low = group * GROUP

                front, back = (low, half + low) if mine else (half + low, low)
                for k in range(3):
                    keep_rest_ref[k * chans + front:k * chans + front + GROUP, :] = total[k]
                    send_rest_ref[k * chans + back:k * chans + back + GROUP, :] = total[3 + k]
                first_ref, rest_ref = (keep_ref, keep_rest_ref) if mine else (send_ref, send_rest_ref)
                first_ref[start + low:start + low + GROUP, :] = total[6]
                rest_ref[3 * chans + low:3 * chans + low + GROUP, :] = total[7]


def share(counts, level_map, s_real, s_imag, prefactor, maxwell):
    blocks, energies, chans = s_real.shape[:3]
    temps = maxwell.shape[0]
    width = energies * GROUP
    first = jax.ShapeDtypeStruct((blocks * chans // 2, chans), jnp.float32)
    rest = jax.ShapeDtypeStruct((3 * chans + chans // 2, chans), jnp.float32)
    hbm = pl.BlockSpec(memory_space=pltpu.HBM)
    vmem = pl.BlockSpec(memory_space=pltpu.VMEM)
    args = (counts, level_map, s_real, s_imag, prefactor, maxwell)
    return pl.pallas_call(
        share_kernel,
        out_shape=[first, first, rest, rest, rest, rest],
        in_specs=[hbm] * 6,
        out_specs=[vmem] * 6,
        scratch_shapes=[
            pltpu.VMEM(s_real.shape, jnp.bfloat16),
            pltpu.VMEM(s_imag.shape, jnp.bfloat16),
            pltpu.SMEM(counts.shape, jnp.int32),
            pltpu.VMEM(level_map.shape, jnp.int32),
            pltpu.VMEM(prefactor.shape, jnp.float32),
            pltpu.VMEM(maxwell.shape, jnp.float32),
            pltpu.VMEM(s_real.shape, jnp.bfloat16),
            pltpu.VMEM((blocks, chans, chans), jnp.bfloat16),
            pltpu.VMEM((blocks, chans, width), jnp.float32),
            pltpu.VMEM((temps * GROUP, width), jnp.float32),
            pltpu.VMEM((temps, width), jnp.float32),
            pltpu.SemaphoreType.DMA((2, blocks, energies // STEP)),
            pltpu.SemaphoreType.DMA((4,)),
        ],
        compiler_params=pltpu.CompilerParams(vmem_limit_bytes=32 * 2**20),
        name="share",
    )(*[pltpu.with_memory_space_constraint(x, pltpu.HBM) for x in args])


def choose_kernel(count_ref, level_ref, picks_ref, columns_ref):
    blocks, rows, chans = picks_ref.shape
    levels = columns_ref.shape[1]
    half = chans // 2
    core = lax.axis_index("core")
    row = iota((rows, chans), 0)
    wanted = row // 2 * 4 + core * 2 + row % 2
    for block in range(blocks):
        seg = jnp.where(iota((1, chans), 1) < count_ref[block], level_ref[pl.ds(block, 1), :], -1)
        columns_ref[block] = jnp.where(iota((levels, chans), 0) == seg, 1.0, 0.0).astype(jnp.bfloat16)
        turned = jnp.concatenate([seg[:, half:], seg[:, :half]], axis=1)
        seg = jnp.where(core == 0, seg, turned)
        picks_ref[block] = jnp.where(wanted == seg, 1.0, 0.0).astype(jnp.bfloat16)


def choose(counts, level_map, levels):
    blocks, chans = level_map.shape
    return pl.pallas_call(
        choose_kernel,
        out_shape=[jax.ShapeDtypeStruct((blocks, levels // 2, chans), jnp.bfloat16),
                   jax.ShapeDtypeStruct((blocks, levels, chans), jnp.bfloat16)],
        in_specs=[pl.BlockSpec(memory_space=pltpu.SMEM), pl.BlockSpec(memory_space=pltpu.VMEM)],
        out_specs=[pl.BlockSpec(memory_space=pltpu.VMEM)] * 2,
        compiler_params=pltpu.CompilerParams(vmem_limit_bytes=16 * 2**20),
        name="choose",
    )(counts, level_map)


def spread_kernel(picks_ref, columns_ref, *refs):
    turn = (((1,), (1,)), ((), ()))
    blocks, _, chans = picks_ref.shape
    half = chans // 2
    total = None
    for block in range(blocks):
        other = refs[blocks + block]
        both = refs[block][...] + jnp.concatenate([other[half:], other[:half]], axis=0)
        hi, lo = split2(both)
        wide = lax.dot_general(jnp.concatenate([hi, lo], axis=0), columns_ref[block], turn,
                               preferred_element_type=jnp.float32)
        hi, lo = split2(wide[:chans] + wide[chans:])
        term = jnp.dot(picks_ref[block], hi, preferred_element_type=jnp.float32)
        term += jnp.dot(picks_ref[block], lo, preferred_element_type=jnp.float32)
        total = term if total is None else total + term
    refs[-1][...] = total


def spread(picks, columns, *parts):
    whole = pl.BlockSpec(memory_space=pltpu.VMEM)
    return pl.pallas_call(
        spread_kernel,
        out_shape=jax.ShapeDtypeStruct((picks.shape[1], columns.shape[1]), jnp.float32),
        in_specs=[whole] * (2 + len(parts)),
        out_specs=whole,
        compiler_params=pltpu.CompilerParams(vmem_limit_bytes=16 * 2**20),
        name="spread",
    )(picks, columns, *parts)


def body(s_real, s_imag, level_map, channel_count, prefactor, maxwell):
    blocks, _, chans = s_real.shape[:3]
    levels = prefactor.shape[0]
    half = chans // 2
    n = lax.axis_size("z")
    swap = [(0, 1), (1, 0)]
    ring = [(2 * i, (i + 1) % n * 2) for i in range(n)]
    ring += [(2 * i + 1, (i - 1) % n * 2 + 1) for i in range(n)]

    def move(x):
        return lax.ppermute(x, ("z", "core"), ring)

    send, keep, *rests = share(channel_count, level_map, s_real, s_imag, prefactor.T, maxwell)
    send_rest, keep_rest = rests[:blocks], rests[blocks:]
    other = lax.ppermute(send, "core", swap)
    mine = []
    for block in range(blocks):
        send_rest[block], other = lax.optimization_barrier((send_rest[block], other))
        other_rest = lax.ppermute(send_rest[block], "core", swap)

        def own(low, high):
            return keep_rest[block][low:high] + other_rest[low:high]

        at = slice(block * half, (block + 1) * half)
        carry = move(keep[at] + other[at])
        first = own(0, chans)
        carry = move(jnp.concatenate([first[:half] + carry, first[half:]]))
        for k in (1, 2):
            carry = move(own(k * chans, (k + 1) * chans) + carry)
        mine.append(jnp.concatenate([own(3 * chans, 3 * chans + half) + carry[:half], carry[half:]]))
    others = [lax.ppermute(x, "core", swap) for x in mine]
    picks, columns = choose(channel_count, level_map, levels)
    part = spread(picks, columns, *mine, *others)
    groups = lax.axis_size("y") * lax.axis_size("x")
    part = part.reshape(groups, levels // 2 // groups, levels)
    part = lax.all_to_all(part, ("y", "x"), 0, 0, tiled=True).sum(0)
    part = lax.all_to_all(part.reshape(n, part.shape[0] // n, levels), "z", 0, 0, tiled=True)
    return jnp.transpose(part, (1, 0, 2))


def solution(mesh):
    fine = Mesh(mesh.devices.reshape(4, 4, 8, 2), ("y", "x", "z", "core"))
    jgrp, energy = ("y", "x"), ("z", "core")
    in_specs = (
        P(jgrp, energy, None, None),
        P(jgrp, energy, None, None),
        P(jgrp, None),
        P(jgrp),
        P(None, energy),
        P(None, energy),
    )
    out_specs = P(("y", "x", "z", "core"), None, None)
    return jax.shard_map(body, mesh=fine, in_specs=in_specs, out_specs=out_specs, check_vma=False)
```

```python
import functools

import jax
import jax.numpy as jnp
from jax import lax
from jax.experimental import pallas as pl
from jax.experimental.pallas import tpu as pltpu
from jax.sharding import Mesh, PartitionSpec as P

PLAN = (((0, 4), (4, 16)), ((0, 16),))
GROUP = 16
LANES = 128
EARLY = 3


def split2(x):
    hi = x.astype(jnp.bfloat16)
    lo = (x - hi.astype(jnp.float32)).astype(jnp.bfloat16)
    return hi, lo


def split3(x):
    hi, mid = split2(x)
    lo = (x - hi.astype(jnp.float32) - mid.astype(jnp.float32)).astype(jnp.bfloat16)
    return hi, mid, lo


def iota(shape, axis):
    return lax.broadcasted_iota(jnp.int32, shape, axis)


def across(x, lanes):
    return jnp.concatenate([x] * (lanes // LANES), axis=1)


def order(z, core):
    sign = 1 - 2 * core
    return [z + sign * 2, z + sign, z - sign * 2, z - sign, z, z + sign * 3, z - sign * 3, z + 4]


def mix(rows_ref, scale_ref, weight, block, at):
    energies, chans = rows_ref.shape[1], rows_ref.shape[3]
    part = rows_ref[block, :, at, :].reshape(energies * GROUP, chans)
    temps = weight.shape[0] // GROUP
    hi, lo = split2(weight * jnp.concatenate([scale_ref[block, at, :]] * temps, axis=0))
    both = jnp.dot(jnp.concatenate([hi, lo], axis=0), part, preferred_element_type=jnp.float32)
    return (both[:temps * GROUP] + both[temps * GROUP:]).reshape(temps, GROUP, chans)


def groups(chans, core):
    half = chans // 2
    for mine in (False, True):
        base = (core if mine else 1 - core) * half
        for low in range(0, half, GROUP):
            yield mine, low, pl.ds(pl.multiple_of(base + low, GROUP), GROUP)


def rows_kernel(count_hbm, level_hbm, real_hbm, imag_hbm, pre_hbm, max_hbm,
                whole_ref, send_ref, keep_ref, send_0, send_1, keep_0, keep_1, rows_ref, scale_ref, weight_ref,
                real_ref, imag_ref, count_ref, level_ref, pre_ref, max_ref,
                same_ref, wide_ref, part_sem, small_sem):
    temps, energies = max_ref.shape
    levels = pre_ref.shape[1]
    blocks, chans = level_ref.shape
    half = chans // 2
    width = energies * GROUP
    smalls = []
    for i, pair in enumerate(((count_hbm, count_ref), (level_hbm, level_ref),
                              (pre_hbm, pre_ref), (max_hbm, max_ref))):
        smalls.append(pltpu.make_async_copy(*pair, small_sem.at[i]))
        smalls[-1].start()
    parts = [[] for _ in range(blocks)]
    for block in range(blocks):
        for step, (low, high) in enumerate(PLAN[block]):
            at = pl.ds(low, high - low)
            parts[block].append([
                pltpu.make_async_copy(x_hbm.at[block, at], x_ref.at[block, at], part_sem.at[i, block, step])
                for i, (x_hbm, x_ref) in enumerate(((real_hbm, real_ref), (imag_hbm, imag_ref)))
            ])
            for copy in parts[block][step]:
                copy.start()
    core = lax.axis_index("core")
    z = lax.axis_index("z")
    jgrp = lax.axis_index("y") * lax.axis_size("x") + lax.axis_index("x")
    delta = jnp.where(iota((LANES, LANES), 0) == iota((LANES, LANES), 1), 1.0, 0.0)
    turn = (((1,), (1,)), ((), ()))
    for copy in smalls[:2]:
        copy.wait()


    seg_cols = []
    for block in range(blocks):
        seg_row = jnp.where(iota((1, chans), 1) < count_ref[block], level_ref[pl.ds(block, 1), :], -1)
        seg_row = seg_row.astype(jnp.float32)
        seg_col = jnp.transpose(jnp.broadcast_to(seg_row, (LANES, chans)))
        same = across(seg_col, chans) == seg_row
        earlier = same & (iota((chans, chans), 1) < iota((chans, chans), 0))
        taken = jnp.dot(jnp.where(earlier, 1.0, 0.0).astype(jnp.bfloat16),
                        jnp.ones((chans, LANES), jnp.bfloat16), preferred_element_type=jnp.float32)
        lead = across(jnp.where((taken == 0.0) & (seg_col >= 0.0), 1.0, 0.0), chans)
        same_ref[block] = jnp.where(same, lead, 0.0).astype(jnp.bfloat16)
        seg_cols.append(seg_col)

    for block in range(blocks):
        factor = (2 * (jgrp * blocks + block) + 1).astype(jnp.float32)
        for step, (low, high) in enumerate(PLAN[block]):
            for copy in parts[block][step]:
                copy.wait()
            for e in range(low, high):
                real = real_ref[block, e].astype(jnp.float32)
                imag = imag_ref[block, e].astype(jnp.float32)
                on = [delta - real[k:k + LANES, k:k + LANES] for k in range(0, chans, LANES)]
                real = jnp.concatenate([
                    jnp.concatenate([on[0], real[:LANES, LANES:]], axis=1),
                    jnp.concatenate([real[LANES:, :LANES], on[1]], axis=1)], axis=0)
                weighted = ((real ** 2 + imag ** 2) * factor).astype(jnp.bfloat16)
                rowsum = jnp.dot(same_ref[block], weighted, preferred_element_type=jnp.float32)
                rows_ref[block, e] = rowsum.astype(jnp.bfloat16)
        if block == 0:
            for copy in smalls[2:]:
                copy.wait()
            spread = iota((3 * energies, width), 1) // GROUP == iota((3 * energies, width), 0) % energies
            spread = jnp.where(spread, 1.0, 0.0).astype(jnp.bfloat16)
            wide_ref[...] = jnp.dot(jnp.concatenate(split3(max_ref[...]), axis=1), spread,
                                    preferred_element_type=jnp.float32)
            hit = iota((GROUP, width), 1) % GROUP == iota((GROUP, width), 0)
            for s, t in enumerate(order(z, core)):
                t = lax.rem(t + temps, temps)
                weight_ref[s * GROUP:(s + 1) * GROUP, :] = jnp.where(hit, wide_ref[pl.ds(t, 1), :], 0.0)
            pre = jnp.concatenate(split3(pre_ref[...]), axis=0)
        picks = across(seg_cols[block], levels) == iota((chans, levels), 1).astype(jnp.float32)
        picks = jnp.where(picks, 1.0, 0.0).astype(jnp.bfloat16)
        own = lax.dot_general(picks, pre, turn, preferred_element_type=jnp.float32)
        scale_ref[block] = jnp.dot(own.astype(jnp.bfloat16), spread, preferred_element_type=jnp.float32)
        weight = weight_ref[(temps - EARLY) * GROUP:, :]
        send_next, keep_next = ((send_0, keep_0), (send_1, keep_1))[block]
        for mine, low, at in groups(chans, core):
            total = mix(rows_ref, scale_ref, weight, block, at)
            front, back = (low, half + low) if mine else (half + low, low)
            keep_next[front:front + GROUP, :] = total[0]
            send_next[back:back + GROUP, :] = total[1]
            if block == 0:
                whole_ref[front:front + GROUP, :] = total[2]
            else:
                (keep_ref if mine else send_ref)[low:low + GROUP, :] = total[2]


def rest_kernel(count_ref, level_ref, rows_ref, scale_ref, weight_ref, *refs):
    picks_ref, columns_ref = refs[-2:]
    blocks, _, chans, _ = rows_ref.shape
    half = chans // 2
    core = lax.axis_index("core")
    weight = weight_ref[:weight_ref.shape[0] - EARLY * GROUP, :]
    for block in range(blocks):
        send_ref, keep_ref = refs[block], refs[blocks + block]
        for mine, low, at in groups(chans, core):
            total = mix(rows_ref, scale_ref, weight, block, at)
            front, back = (low, half + low) if mine else (half + low, low)
            for k in range(2):
                keep_ref[k * chans + front:k * chans + front + GROUP, :] = total[k]
                send_ref[k * chans + back:k * chans + back + GROUP, :] = total[2 + k]
            (keep_ref if mine else send_ref)[2 * chans + low:2 * chans + low + GROUP, :] = total[4]

    levels = columns_ref.shape[1]
    row = iota((levels // 2, chans), 0)
    wanted = row // 2 * 4 + core * 2 + row % 2
    for block in range(blocks):
        seg = jnp.where(iota((1, chans), 1) < count_ref[block], level_ref[pl.ds(block, 1), :], -1)
        columns_ref[block] = jnp.where(iota((levels, chans), 0) == seg, 1.0, 0.0).astype(jnp.bfloat16)
        turned = jnp.concatenate([seg[:, half:], seg[:, :half]], axis=1)
        seg = jnp.where(core == 0, seg, turned)
        picks_ref[block] = jnp.where(wanted == seg, 1.0, 0.0).astype(jnp.bfloat16)


def rows(counts, level_map, s_real, s_imag, prefactor, maxwell):
    blocks, energies, chans = s_real.shape[:3]
    temps = maxwell.shape[0]
    width = energies * GROUP
    first = jax.ShapeDtypeStruct((chans // 2, chans), jnp.float32)
    second = jax.ShapeDtypeStruct((chans, chans), jnp.float32)
    hbm = pl.BlockSpec(memory_space=pltpu.HBM)
    vmem = pl.BlockSpec(memory_space=pltpu.VMEM)
    args = (counts, level_map, s_real, s_imag, prefactor, maxwell)
    return pl.pallas_call(
        rows_kernel,
        out_shape=[second] + [first] * 2 + [second] * (2 * blocks) + [
                   jax.ShapeDtypeStruct(s_real.shape, jnp.bfloat16),
                   jax.ShapeDtypeStruct((blocks, chans, width), jnp.float32),
                   jax.ShapeDtypeStruct((temps * GROUP, width), jnp.float32)],
        in_specs=[hbm] * 6,
        out_specs=[vmem] * (6 + 2 * blocks),
        scratch_shapes=[
            pltpu.VMEM(s_real.shape, jnp.bfloat16),
            pltpu.VMEM(s_imag.shape, jnp.bfloat16),
            pltpu.SMEM(counts.shape, jnp.int32),
            pltpu.VMEM(level_map.shape, jnp.int32),
            pltpu.VMEM(prefactor.shape, jnp.float32),
            pltpu.VMEM(maxwell.shape, jnp.float32),
            pltpu.VMEM((blocks, chans, chans), jnp.bfloat16),
            pltpu.VMEM((temps, width), jnp.float32),
            pltpu.SemaphoreType.DMA((2, blocks, len(PLAN[0]))),
            pltpu.SemaphoreType.DMA((4,)),
        ],
        compiler_params=pltpu.CompilerParams(vmem_limit_bytes=24 * 2**20),
        name="rows",
    )(*[pltpu.with_memory_space_constraint(x, pltpu.HBM) for x in args])


def rest(counts, level_map, levels, rows, scale, weight):
    blocks, _, chans, _ = rows.shape
    out = jax.ShapeDtypeStruct((2 * chans + chans // 2, chans), jnp.float32)
    vmem = pl.BlockSpec(memory_space=pltpu.VMEM)
    *out, picks, columns = pl.pallas_call(
        rest_kernel,
        out_shape=[out] * (2 * blocks) + [jax.ShapeDtypeStruct((blocks, levels // 2, chans), jnp.bfloat16),
                                          jax.ShapeDtypeStruct((blocks, levels, chans), jnp.bfloat16)],
        in_specs=[pl.BlockSpec(memory_space=pltpu.SMEM)] + [vmem] * 4,
        out_specs=[vmem] * (2 * blocks + 2),
        compiler_params=pltpu.CompilerParams(vmem_limit_bytes=24 * 2**20),
        name="rest",
    )(counts, level_map, rows, scale, weight)
    return out[:blocks], out[blocks:], picks, columns


def spread_kernel(picks_ref, columns_ref, *refs):
    turn = (((1,), (1,)), ((), ()))
    blocks, _, chans = picks_ref.shape
    half = chans // 2
    total = None
    for block in range(blocks):
        other = refs[blocks + block]
        both = refs[block][...] + jnp.concatenate([other[half:], other[:half]], axis=0)
        hi, lo = split2(both)
        wide = lax.dot_general(jnp.concatenate([hi, lo], axis=0), columns_ref[block], turn,
                               preferred_element_type=jnp.float32)
        hi, lo = split2(wide[:chans] + wide[chans:])
        term = jnp.dot(picks_ref[block], hi, preferred_element_type=jnp.float32)
        term += jnp.dot(picks_ref[block], lo, preferred_element_type=jnp.float32)
        total = term if total is None else total + term
    refs[-1][...] = total


def spread(picks, columns, *parts):
    whole = pl.BlockSpec(memory_space=pltpu.VMEM)
    return pl.pallas_call(
        spread_kernel,
        out_shape=jax.ShapeDtypeStruct((picks.shape[1], columns.shape[1]), jnp.float32),
        in_specs=[whole] * (2 + len(parts)),
        out_specs=whole,
        compiler_params=pltpu.CompilerParams(vmem_limit_bytes=16 * 2**20),
        name="spread",
    )(picks, columns, *parts)


def body(s_real, s_imag, level_map, channel_count, prefactor, maxwell):
    blocks, _, chans = s_real.shape[:3]
    levels = prefactor.shape[0]
    half = chans // 2
    n = lax.axis_size("z")
    swap = [(0, 1), (1, 0)]
    ring = [(2 * i, (i + 1) % n * 2) for i in range(n)]
    ring += [(2 * i + 1, (i - 1) % n * 2 + 1) for i in range(n)]

    def move(x):
        return lax.ppermute(x, ("z", "core"), ring)

    whole, send, keep, *held = rows(channel_count, level_map, s_real, s_imag, prefactor.T, maxwell)
    send_next, keep_next, held = held[:blocks], held[blocks:2 * blocks], held[2 * blocks:]
    other = lax.ppermute(send, "core", swap)
    send_next, other = lax.optimization_barrier((send_next, other))
    nexts = [x + lax.ppermute(y, "core", swap) for x, y in zip(keep_next, send_next)]
    held[0], first = lax.optimization_barrier((held[0], keep + other))
    carries = [move(whole), move(first)]
    send_rest, keep_rest, picks, columns = rest(channel_count, level_map, levels, *held)
    carries[0], send_rest = lax.optimization_barrier((carries[0], send_rest))
    others_rest = [lax.ppermute(x, "core", swap) for x in send_rest]
    mine = []
    for block, carry in enumerate(carries):
        if block == 0:
            carry = nexts[block] + carry
        else:
            carry = jnp.concatenate([nexts[block][:half] + carry, nexts[block][half:]])
        other_rest = others_rest[block]

        def own(low, high):
            return keep_rest[block][low:high] + other_rest[low:high]

        carry = move(carry)
        for k in range(2):
            carry = move(own(k * chans, (k + 1) * chans) + carry)
        mine.append(jnp.concatenate([own(2 * chans, 2 * chans + half) + carry[:half], carry[half:]]))
    others = [lax.ppermute(x, "core", swap) for x in mine]
    part = spread(picks, columns, *mine, *others)
    size = lax.axis_size("y") * lax.axis_size("x")
    part = part.reshape(size, levels // 2 // size, levels)
    part = lax.all_to_all(part, ("y", "x"), 0, 0, tiled=True).sum(0)
    part = lax.all_to_all(part.reshape(n, part.shape[0] // n, levels), "z", 0, 0, tiled=True)
    return jnp.transpose(part, (1, 0, 2))


def solution(mesh):
    fine = Mesh(mesh.devices.reshape(4, 4, 8, 2), ("y", "x", "z", "core"))
    jgrp, energy = ("y", "x"), ("z", "core")
    in_specs = (
        P(jgrp, energy, None, None),
        P(jgrp, energy, None, None),
        P(jgrp, None),
        P(jgrp),
        P(None, energy),
        P(None, energy),
    )
    out_specs = P(("y", "x", "z", "core"), None, None)
    return jax.shard_map(body, mesh=fine, in_specs=in_specs, out_specs=out_specs, check_vma=False)
```

```python
import functools

import jax
import jax.numpy as jnp
from jax import lax
from jax.experimental import pallas as pl
from jax.experimental.pallas import tpu as pltpu
from jax.sharding import Mesh, PartitionSpec as P

PLAN = (((0, 4), (4, 16)), ((0, 16),))
GROUP = 16
LANES = 128


def split2(x):
    hi = x.astype(jnp.bfloat16)
    lo = (x - hi.astype(jnp.float32)).astype(jnp.bfloat16)
    return hi, lo


def split3(x):
    hi, mid = split2(x)
    lo = (x - hi.astype(jnp.float32) - mid.astype(jnp.float32)).astype(jnp.bfloat16)
    return hi, mid, lo


def iota(shape, axis):
    return lax.broadcasted_iota(jnp.int32, shape, axis)


def across(x, lanes):
    return jnp.concatenate([x] * (lanes // LANES), axis=1)


def order(z, core):
    sign = 1 - 2 * core
    return [z + sign, z + sign + 4, z - sign, z - sign + 4, z, z + 4, z + 2 * sign, z - 2 * sign]


def mix(rows_ref, scale_ref, weight, at):
    energies, _, chans = rows_ref.shape
    part = rows_ref[:, at, :].reshape(energies * GROUP, chans)
    temps = weight.shape[0] // GROUP
    hi, lo = split2(weight * jnp.concatenate([scale_ref[at, :]] * temps, axis=0))
    both = jnp.dot(jnp.concatenate([hi, lo], axis=0), part, preferred_element_type=jnp.float32)
    return (both[:temps * GROUP] + both[temps * GROUP:]).reshape(temps, GROUP, chans)


def groups(chans, core):
    half = chans // 2
    for mine in (False, True):
        base = (core if mine else 1 - core) * half
        for low in range(0, half, GROUP):
            at = pl.ds(pl.multiple_of(base + low, GROUP), GROUP)
            yield (low, half + low, at) if mine else (half + low, low, at)


def spread_lanes(energies):
    shape = (3 * energies, energies * GROUP)
    hit = iota(shape, 1) // GROUP == iota(shape, 0) % energies
    return jnp.where(hit, 1.0, 0.0).astype(jnp.bfloat16)


def leaders(block, count_ref, level_ref):
    chans = level_ref.shape[1]
    seg_row = jnp.where(iota((1, chans), 1) < count_ref[block], level_ref[pl.ds(block, 1), :], -1)
    seg_row = seg_row.astype(jnp.float32)
    seg_col = jnp.transpose(jnp.broadcast_to(seg_row, (LANES, chans)))
    same = across(seg_col, chans) == seg_row
    earlier = same & (iota((chans, chans), 1) < iota((chans, chans), 0))
    taken = jnp.dot(jnp.where(earlier, 1.0, 0.0).astype(jnp.bfloat16),
                    jnp.ones((chans, LANES), jnp.bfloat16), preferred_element_type=jnp.float32)
    lead = across(jnp.where((taken == 0.0) & (seg_col >= 0.0), 1.0, 0.0), chans)
    return seg_col, jnp.where(same, lead, 0.0).astype(jnp.bfloat16)


def scales(seg_col, pre_ref):
    energies, levels = pre_ref.shape
    picks = across(seg_col, levels) == iota((seg_col.shape[0], levels), 1).astype(jnp.float32)
    picks = jnp.where(picks, 1.0, 0.0).astype(jnp.bfloat16)
    own = lax.dot_general(picks, jnp.concatenate(split3(pre_ref[...]), axis=0), (((1,), (1,)), ((), ())),
                          preferred_element_type=jnp.float32)
    return jnp.dot(own.astype(jnp.bfloat16), spread_lanes(energies), preferred_element_type=jnp.float32)


def rowsums(block, blocks, energies, real_ref, imag_ref, same_ref, rows_ref):
    chans = same_ref.shape[0]
    jgrp = lax.axis_index("y") * lax.axis_size("x") + lax.axis_index("x")
    factor = (2 * (jgrp * blocks + block) + 1).astype(jnp.float32)
    delta = jnp.where(iota((LANES, LANES), 0) == iota((LANES, LANES), 1), 1.0, 0.0)
    for e in energies:
        real = real_ref[e].astype(jnp.float32)
        imag = imag_ref[e].astype(jnp.float32)
        on = [delta - real[k:k + LANES, k:k + LANES] for k in range(0, chans, LANES)]
        real = jnp.concatenate([
            jnp.concatenate([on[0], real[:LANES, LANES:]], axis=1),
            jnp.concatenate([real[LANES:, :LANES], on[1]], axis=1)], axis=0)
        weighted = ((real ** 2 + imag ** 2) * factor).astype(jnp.bfloat16)
        rowsum = jnp.dot(same_ref[...], weighted, preferred_element_type=jnp.float32)
        rows_ref[e] = rowsum.astype(jnp.bfloat16)


def share_kernel(count_hbm, level_hbm, real_hbm, imag_hbm, pre_hbm, max_hbm, *refs):
    blocks, chans = level_hbm.shape
    outs, refs = refs[:5 * blocks], refs[5 * blocks:]
    (real_ref, imag_ref, count_ref, level_ref, pre_ref, max_ref,
     rows_ref, same_ref, scale_ref, weight_ref, wide_ref, part_sem, small_sem) = refs
    temps, energies = max_ref.shape
    half = chans // 2
    width = energies * GROUP
    core = lax.axis_index("core")
    smalls = []
    for i, pair in enumerate(((count_hbm, count_ref), (level_hbm, level_ref),
                              (pre_hbm, pre_ref), (max_hbm, max_ref))):
        smalls.append(pltpu.make_async_copy(*pair, small_sem.at[i]))
        smalls[-1].start()
    parts = [[] for _ in range(blocks)]
    for block in range(blocks):
        for step, (low, high) in enumerate(PLAN[block]):
            at = pl.ds(low, high - low)
            parts[block].append([
                pltpu.make_async_copy(x_hbm.at[block, at], x_ref.at[block, at], part_sem.at[i, block, step])
                for i, (x_hbm, x_ref) in enumerate(((real_hbm, real_ref), (imag_hbm, imag_ref)))
            ])
            for copy in parts[block][step]:
                copy.start()
    for copy in smalls[:2]:
        copy.wait()
    seg_cols = []
    for block in range(blocks):
        seg_col, same_ref[block] = leaders(block, count_ref, level_ref)
        seg_cols.append(seg_col)
    for block in range(blocks):
        for (low, high), copies in zip(PLAN[block], parts[block]):
            for copy in copies:
                copy.wait()
            rowsums(block, blocks, range(low, high), real_ref.at[block], imag_ref.at[block],
                    same_ref.at[block], rows_ref.at[block])
        if block == 0:
            for copy in smalls[2:]:
                copy.wait()
            wide_ref[...] = jnp.dot(jnp.concatenate(split3(max_ref[...]), axis=1), spread_lanes(energies),
                                    preferred_element_type=jnp.float32)
            hit = iota((GROUP, width), 1) % GROUP == iota((GROUP, width), 0)
            for s, t in enumerate(order(lax.axis_index("z"), core)):
                t = lax.rem(t + temps, temps)
                weight_ref[s * GROUP:(s + 1) * GROUP, :] = jnp.where(hit, wide_ref[pl.ds(t, 1), :], 0.0)
        scale_ref[block] = scales(seg_cols[block], pre_ref)
        send_ref, keep_ref, send_near, keep_near, own_ref = outs[block::blocks]
        for front, back, at in groups(chans, core):
            total = mix(rows_ref.at[block], scale_ref.at[block], weight_ref[...], at)
            low, mine = front % half, front < half
            for k in range(2):
                keep_near[k * chans + front:k * chans + front + GROUP, :] = total[k]
                send_near[k * chans + back:k * chans + back + GROUP, :] = total[2 + k]
                own_ref[k * chans + front:k * chans + front + GROUP, :] = total[4 + k]
                first_ref = keep_ref if mine else send_ref
                first_ref[k * half + low:k * half + low + GROUP, :] = total[6 + k if mine else 7 - k]


def choose_kernel(count_ref, level_ref, picks_ref, columns_ref):
    blocks, chans = level_ref.shape
    half = chans // 2
    core = lax.axis_index("core")
    levels = columns_ref.shape[1]
    row = iota((levels // 2, chans), 0)
    wanted = row // 2 * 4 + core * 2 + row % 2
    for block in range(blocks):
        seg = jnp.where(iota((1, chans), 1) < count_ref[block], level_ref[pl.ds(block, 1), :], -1)
        columns_ref[block] = jnp.where(iota((levels, chans), 0) == seg, 1.0, 0.0).astype(jnp.bfloat16)
        turned = jnp.concatenate([seg[:, half:], seg[:, :half]], axis=1)
        seg = jnp.where(core == 0, seg, turned)
        picks_ref[block] = jnp.where(wanted == seg, 1.0, 0.0).astype(jnp.bfloat16)


def float_of(*shape):
    return jax.ShapeDtypeStruct(shape, jnp.float32)


def half_of(*shape):
    return jax.ShapeDtypeStruct(shape, jnp.bfloat16)


def share(counts, level_map, s_real, s_imag, prefactor, maxwell):
    blocks, energies, chans = s_real.shape[:3]
    temps = maxwell.shape[0]
    width = energies * GROUP
    args = (counts, level_map, s_real, s_imag, prefactor, maxwell)
    out = pl.pallas_call(
        share_kernel,
        out_shape=[float_of(chans, chans)] * (2 * blocks) + [float_of(2 * chans, chans)] * (3 * blocks),
        in_specs=[pl.BlockSpec(memory_space=pltpu.HBM)] * 6,
        out_specs=[pl.BlockSpec(memory_space=pltpu.VMEM)] * (5 * blocks),
        scratch_shapes=[
            pltpu.VMEM(s_real.shape, jnp.bfloat16),
            pltpu.VMEM(s_imag.shape, jnp.bfloat16),
            pltpu.SMEM(counts.shape, jnp.int32),
            pltpu.VMEM(level_map.shape, jnp.int32),
            pltpu.VMEM(prefactor.shape, jnp.float32),
            pltpu.VMEM(maxwell.shape, jnp.float32),
            pltpu.VMEM(s_real.shape, jnp.bfloat16),
            pltpu.VMEM((blocks, chans, chans), jnp.bfloat16),
            pltpu.VMEM((blocks, chans, width), jnp.float32),
            pltpu.VMEM((temps * GROUP, width), jnp.float32),
            pltpu.VMEM((temps, width), jnp.float32),
            pltpu.SemaphoreType.DMA((2, blocks, 2)),
            pltpu.SemaphoreType.DMA((4,)),
        ],
        compiler_params=pltpu.CompilerParams(vmem_limit_bytes=24 * 2**20),
        name="share",
    )(*[pltpu.with_memory_space_constraint(x, pltpu.HBM) for x in args])
    return [out[i * blocks:(i + 1) * blocks] for i in range(5)]


def choose(counts, level_map, levels):
    blocks, chans = level_map.shape
    return pl.pallas_call(
        choose_kernel,
        out_shape=[half_of(blocks, levels // 2, chans), half_of(blocks, levels, chans)],
        in_specs=[pl.BlockSpec(memory_space=pltpu.SMEM), pl.BlockSpec(memory_space=pltpu.VMEM)],
        out_specs=[pl.BlockSpec(memory_space=pltpu.VMEM)] * 2,
        compiler_params=pltpu.CompilerParams(vmem_limit_bytes=16 * 2**20),
        name="choose",
    )(counts, level_map)


def spread_kernel(block, picks_ref, columns_ref, mine_ref, other_ref, *refs):
    out_ref = refs[-1]
    size, share = out_ref.shape[0], out_ref.shape[1] // 2
    chans = columns_ref.shape[2]
    half = chans // 2
    for k in range(2):
        low = k * chans
        both = mine_ref[low:low + chans] + jnp.concatenate(
            [other_ref[low + half:low + chans], other_ref[low:low + half]], axis=0)
        hi, lo = split2(both)
        wide = lax.dot_general(jnp.concatenate([hi, lo], axis=0), columns_ref[block], (((1,), (1,)), ((), ())),
                               preferred_element_type=jnp.float32)
        hi, lo = split2(wide[:chans] + wide[chans:])
        term = jnp.dot(picks_ref[block], hi, preferred_element_type=jnp.float32)
        term += jnp.dot(picks_ref[block], lo, preferred_element_type=jnp.float32)
        term = term.reshape(size, share, -1)
        at = slice(k * share, (k + 1) * share)
        out_ref[:, at, :] = term if len(refs) == 1 else refs[0][:, at, :] + term


def spread(block, size, picks, columns, *parts):
    whole = pl.BlockSpec(memory_space=pltpu.VMEM)
    rows, levels = picks.shape[1], columns.shape[1]
    return pl.pallas_call(
        functools.partial(spread_kernel, block),
        out_shape=float_of(size, 2 * rows // size, levels),
        in_specs=[whole] * (2 + len(parts)),
        out_specs=whole,
        compiler_params=pltpu.CompilerParams(vmem_limit_bytes=16 * 2**20),
        name="spread",
    )(picks, columns, *parts)


def body(s_real, s_imag, level_map, channel_count, prefactor, maxwell):
    chans, levels = s_real.shape[2], prefactor.shape[0]
    half = chans // 2
    n = lax.axis_size("z")
    size = lax.axis_size("y") * lax.axis_size("x")
    swap = [(0, 1), (1, 0)]
    ring = [(2 * i, (i + 1) % n * 2) for i in range(n)]
    ring += [(2 * i + 1, (i - 1) % n * 2 + 1) for i in range(n)]

    def move(x):
        return lax.ppermute(x, ("z", "core"), ring)

    send, keep, send_near, keep_near, own = share(
        channel_count, level_map, s_real, s_imag, prefactor.T, maxwell)
    others = [lax.ppermute(x, "core", swap) for x in send]
    send_near, others = lax.optimization_barrier((send_near, others))
    mine = []
    for block in range(len(send)):
        carry = move(keep[block] + others[block])
        near = keep_near[block] + lax.ppermute(send_near[block], "core", swap)
        carry = move(jnp.concatenate([near[:half] + carry[:half], near[half:chans],
                                      near[chans:chans + half] + carry[half:], near[chans + half:]]))
        mine.append(carry + own[block])
    others = [lax.ppermute(x, "core", swap) for x in mine]
    picks, columns = choose(channel_count, level_map, levels)
    part = spread(0, size, picks, columns, mine[0], others[0])
    part = spread(1, size, picks, columns, mine[1], others[1], part)
    part = lax.all_to_all(part, ("y", "x"), 0, 0, tiled=True).sum(0)
    part = part.reshape(2, n, -1, levels).transpose(1, 0, 2, 3)
    part = lax.all_to_all(part, "z", 0, 0, tiled=True)
    part = part[:, 0] + jnp.roll(part[:, 1], 4, axis=0)
    return jnp.transpose(part, (1, 0, 2))


def solution(mesh):
    fine = Mesh(mesh.devices.reshape(4, 4, 8, 2), ("y", "x", "z", "core"))
    jgrp, energy = ("y", "x"), ("z", "core")
    in_specs = (
        P(jgrp, energy, None, None),
        P(jgrp, energy, None, None),
        P(jgrp, None),
        P(jgrp),
        P(None, energy),
        P(None, energy),
    )
    out_specs = P(("y", "x", "z", "core"), None, None)
    return jax.shard_map(body, mesh=fine, in_specs=in_specs, out_specs=out_specs, check_vma=False)
```

```python
import functools

import jax
import jax.numpy as jnp
from jax import lax
from jax.experimental import pallas as pl
from jax.experimental.pallas import tpu as pltpu
from jax.sharding import Mesh, PartitionSpec as P

PLAN = (((0, 4), (4, 16)), ((0, 16),))
GROUP = 16
LANES = 128


def split2(x):
    hi = x.astype(jnp.bfloat16)
    lo = (x - hi.astype(jnp.float32)).astype(jnp.bfloat16)
    return hi, lo


def split3(x):
    hi, mid = split2(x)
    lo = (x - hi.astype(jnp.float32) - mid.astype(jnp.float32)).astype(jnp.bfloat16)
    return hi, mid, lo


def iota(shape, axis):
    return lax.broadcasted_iota(jnp.int32, shape, axis)


def across(x, lanes):
    return jnp.concatenate([x] * (lanes // LANES), axis=1)


def order(z, core):
    sign = 1 - 2 * core
    return [z + sign, z + sign + 4, z - sign, z - sign + 4, z, z + 4, z + 2 * sign, z - 2 * sign]


def mix(rows_ref, scale_ref, weight, at):
    energies, _, chans = rows_ref.shape
    part = rows_ref[:, at, :].reshape(energies * GROUP, chans)
    temps = weight.shape[0] // GROUP
    hi, lo = split2(weight * jnp.concatenate([scale_ref[at, :]] * temps, axis=0))
    both = jnp.dot(jnp.concatenate([hi, lo], axis=0), part, preferred_element_type=jnp.float32)
    return (both[:temps * GROUP] + both[temps * GROUP:]).reshape(temps, GROUP, chans)


def groups(chans, core):
    half = chans // 2
    for mine in (False, True):
        base = (core if mine else 1 - core) * half
        for low in range(0, half, GROUP):
            at = pl.ds(pl.multiple_of(base + low, GROUP), GROUP)
            yield (low, half + low, at) if mine else (half + low, low, at)


def spread_lanes(energies):
    shape = (3 * energies, energies * GROUP)
    hit = iota(shape, 1) // GROUP == iota(shape, 0) % energies
    return jnp.where(hit, 1.0, 0.0).astype(jnp.bfloat16)


def leaders(block, count_ref, level_ref):
    chans = level_ref.shape[1]
    seg_row = jnp.where(iota((1, chans), 1) < count_ref[block], level_ref[pl.ds(block, 1), :], -1)
    seg_row = seg_row.astype(jnp.float32)
    seg_col = jnp.transpose(jnp.broadcast_to(seg_row, (LANES, chans)))
    same = across(seg_col, chans) == seg_row
    earlier = same & (iota((chans, chans), 1) < iota((chans, chans), 0))
    taken = jnp.dot(jnp.where(earlier, 1.0, 0.0).astype(jnp.bfloat16),
                    jnp.ones((chans, LANES), jnp.bfloat16), preferred_element_type=jnp.float32)
    lead = across(jnp.where((taken == 0.0) & (seg_col >= 0.0), 1.0, 0.0), chans)
    return seg_col, jnp.where(same, lead, 0.0).astype(jnp.bfloat16)


def scales(seg_col, pre_ref):
    energies, levels = pre_ref.shape
    picks = across(seg_col, levels) == iota((seg_col.shape[0], levels), 1).astype(jnp.float32)
    picks = jnp.where(picks, 1.0, 0.0).astype(jnp.bfloat16)
    own = lax.dot_general(picks, jnp.concatenate(split3(pre_ref[...]), axis=0), (((1,), (1,)), ((), ())),
                          preferred_element_type=jnp.float32)
    return jnp.dot(own.astype(jnp.bfloat16), spread_lanes(energies), preferred_element_type=jnp.float32)


def rowsums(block, blocks, energies, real_ref, imag_ref, same_ref, rows_ref):
    chans = same_ref.shape[0]
    jgrp = lax.axis_index("y") * lax.axis_size("x") + lax.axis_index("x")
    factor = (2 * (jgrp * blocks + block) + 1).astype(jnp.float32)
    delta = jnp.where(iota((LANES, LANES), 0) == iota((LANES, LANES), 1), 1.0, 0.0)
    for e in energies:
        real = real_ref[e].astype(jnp.float32)
        imag = imag_ref[e].astype(jnp.float32)
        on = [delta - real[k:k + LANES, k:k + LANES] for k in range(0, chans, LANES)]
        real = jnp.concatenate([
            jnp.concatenate([on[0], real[:LANES, LANES:]], axis=1),
            jnp.concatenate([real[LANES:, :LANES], on[1]], axis=1)], axis=0)
        weighted = ((real ** 2 + imag ** 2) * factor).astype(jnp.bfloat16)
        rowsum = jnp.dot(same_ref[...], weighted, preferred_element_type=jnp.float32)
        rows_ref[e] = rowsum.astype(jnp.bfloat16)


def share_kernel(count_hbm, level_hbm, real_hbm, imag_hbm, pre_hbm, max_hbm, *refs):
    blocks, chans = level_hbm.shape
    outs, refs = refs[:5 * blocks], refs[5 * blocks:]
    (real_ref, imag_ref, count_ref, level_ref, pre_ref, max_ref,
     rows_ref, same_ref, scale_ref, weight_ref, wide_ref, part_sem, small_sem) = refs
    temps, energies = max_ref.shape
    half = chans // 2
    width = energies * GROUP
    core = lax.axis_index("core")
    smalls = []
    for i, pair in enumerate(((count_hbm, count_ref), (level_hbm, level_ref),
                              (pre_hbm, pre_ref), (max_hbm, max_ref))):
        smalls.append(pltpu.make_async_copy(*pair, small_sem.at[i]))
        smalls[-1].start()
    parts = [[] for _ in range(blocks)]
    for block in range(blocks):
        for step, (low, high) in enumerate(PLAN[block]):
            at = pl.ds(low, high - low)
            parts[block].append([
                pltpu.make_async_copy(x_hbm.at[block, at], x_ref.at[block, at], part_sem.at[i, block, step])
                for i, (x_hbm, x_ref) in enumerate(((real_hbm, real_ref), (imag_hbm, imag_ref)))
            ])
            for copy in parts[block][step]:
                copy.start()
    for copy in smalls[:2]:
        copy.wait()
    seg_cols = []
    for block in range(blocks):
        seg_col, same_ref[block] = leaders(block, count_ref, level_ref)
        seg_cols.append(seg_col)
    for block in range(blocks):
        for (low, high), copies in zip(PLAN[block], parts[block]):
            for copy in copies:
                copy.wait()
            rowsums(block, blocks, range(low, high), real_ref.at[block], imag_ref.at[block],
                    same_ref.at[block], rows_ref.at[block])
        if block == 0:
            for copy in smalls[2:]:
                copy.wait()
            wide_ref[...] = jnp.dot(jnp.concatenate(split3(max_ref[...]), axis=1), spread_lanes(energies),
                                    preferred_element_type=jnp.float32)
            hit = iota((GROUP, width), 1) % GROUP == iota((GROUP, width), 0)
            for s, t in enumerate(order(lax.axis_index("z"), core)):
                t = lax.rem(t + temps, temps)
                weight_ref[s * GROUP:(s + 1) * GROUP, :] = jnp.where(hit, wide_ref[pl.ds(t, 1), :], 0.0)
    for block in range(blocks):
        scale_ref[block] = scales(seg_cols[block], pre_ref)
        send_ref, keep_ref, send_near, keep_near, own_ref = outs[block::blocks]
        for front, back, at in groups(chans, core):
            total = mix(rows_ref.at[block], scale_ref.at[block], weight_ref[...], at)
            low, mine = front % half, front < half
            for k in range(2):
                keep_near[k * chans + front:k * chans + front + GROUP, :] = total[k]
                send_near[k * chans + back:k * chans + back + GROUP, :] = total[2 + k]
                own_ref[k * chans + front:k * chans + front + GROUP, :] = total[4 + k]
                first_ref = keep_ref if mine else send_ref
                first_ref[k * half + low:k * half + low + GROUP, :] = total[6 + k if mine else 7 - k]


def choose_kernel(count_ref, level_ref, picks_ref, columns_ref):
    blocks, chans = level_ref.shape
    half = chans // 2
    core = lax.axis_index("core")
    levels = columns_ref.shape[1]
    row = iota((levels // 2, chans), 0)
    wanted = row // 2 * 4 + core * 2 + row % 2
    for block in range(blocks):
        seg = jnp.where(iota((1, chans), 1) < count_ref[block], level_ref[pl.ds(block, 1), :], -1)
        columns_ref[block] = jnp.where(iota((levels, chans), 0) == seg, 1.0, 0.0).astype(jnp.bfloat16)
        turned = jnp.concatenate([seg[:, half:], seg[:, :half]], axis=1)
        seg = jnp.where(core == 0, seg, turned)
        picks_ref[block] = jnp.where(wanted == seg, 1.0, 0.0).astype(jnp.bfloat16)


def float_of(*shape):
    return jax.ShapeDtypeStruct(shape, jnp.float32)


def half_of(*shape):
    return jax.ShapeDtypeStruct(shape, jnp.bfloat16)


def share(counts, level_map, s_real, s_imag, prefactor, maxwell):
    blocks, energies, chans = s_real.shape[:3]
    temps = maxwell.shape[0]
    width = energies * GROUP
    args = (counts, level_map, s_real, s_imag, prefactor, maxwell)
    out = pl.pallas_call(
        share_kernel,
        out_shape=[float_of(chans, chans)] * (2 * blocks) + [float_of(2 * chans, chans)] * (3 * blocks),
        in_specs=[pl.BlockSpec(memory_space=pltpu.HBM)] * 6,
        out_specs=[pl.BlockSpec(memory_space=pltpu.VMEM)] * (5 * blocks),
        scratch_shapes=[
            pltpu.VMEM(s_real.shape, jnp.bfloat16),
            pltpu.VMEM(s_imag.shape, jnp.bfloat16),
            pltpu.SMEM(counts.shape, jnp.int32),
            pltpu.VMEM(level_map.shape, jnp.int32),
            pltpu.VMEM(prefactor.shape, jnp.float32),
            pltpu.VMEM(maxwell.shape, jnp.float32),
            pltpu.VMEM(s_real.shape, jnp.bfloat16),
            pltpu.VMEM((blocks, chans, chans), jnp.bfloat16),
            pltpu.VMEM((blocks, chans, width), jnp.float32),
            pltpu.VMEM((temps * GROUP, width), jnp.float32),
            pltpu.VMEM((temps, width), jnp.float32),
            pltpu.SemaphoreType.DMA((2, blocks, 2)),
            pltpu.SemaphoreType.DMA((4,)),
        ],
        compiler_params=pltpu.CompilerParams(vmem_limit_bytes=24 * 2**20),
        name="share",
    )(*[pltpu.with_memory_space_constraint(x, pltpu.HBM) for x in args])
    return [out[i * blocks:(i + 1) * blocks] for i in range(5)]


def choose(counts, level_map, levels):
    blocks, chans = level_map.shape
    return pl.pallas_call(
        choose_kernel,
        out_shape=[half_of(blocks, levels // 2, chans), half_of(blocks, levels, chans)],
        in_specs=[pl.BlockSpec(memory_space=pltpu.SMEM), pl.BlockSpec(memory_space=pltpu.VMEM)],
        out_specs=[pl.BlockSpec(memory_space=pltpu.VMEM)] * 2,
        compiler_params=pltpu.CompilerParams(vmem_limit_bytes=16 * 2**20),
        name="choose",
    )(counts, level_map)


def spread_kernel(block, picks_ref, columns_ref, mine_ref, other_ref, *refs):
    out_ref = refs[-1]
    size, share = out_ref.shape[0], out_ref.shape[1] // 2
    chans = columns_ref.shape[2]
    half = chans // 2
    for k in range(2):
        low = k * chans
        both = mine_ref[low:low + chans] + jnp.concatenate(
            [other_ref[low + half:low + chans], other_ref[low:low + half]], axis=0)
        hi, lo = split2(both)
        wide = lax.dot_general(jnp.concatenate([hi, lo], axis=0), columns_ref[block], (((1,), (1,)), ((), ())),
                               preferred_element_type=jnp.float32)
        hi, lo = split2(wide[:chans] + wide[chans:])
        term = jnp.dot(picks_ref[block], hi, preferred_element_type=jnp.float32)
        term += jnp.dot(picks_ref[block], lo, preferred_element_type=jnp.float32)
        term = term.reshape(size, share, -1)
        at = slice(k * share, (k + 1) * share)
        out_ref[:, at, :] = term if len(refs) == 1 else refs[0][:, at, :] + term


def spread(block, size, picks, columns, *parts):
    whole = pl.BlockSpec(memory_space=pltpu.VMEM)
    rows, levels = picks.shape[1], columns.shape[1]
    return pl.pallas_call(
        functools.partial(spread_kernel, block),
        out_shape=float_of(size, 2 * rows // size, levels),
        in_specs=[whole] * (2 + len(parts)),
        out_specs=whole,
        compiler_params=pltpu.CompilerParams(vmem_limit_bytes=16 * 2**20),
        name="spread",
    )(picks, columns, *parts)


def body(s_real, s_imag, level_map, channel_count, prefactor, maxwell):
    chans, levels = s_real.shape[2], prefactor.shape[0]
    half = chans // 2
    n = lax.axis_size("z")
    size = lax.axis_size("y") * lax.axis_size("x")
    swap = [(0, 1), (1, 0)]
    ring = [(2 * i, (i + 1) % n * 2) for i in range(n)]
    ring += [(2 * i + 1, (i - 1) % n * 2 + 1) for i in range(n)]

    def move(x):
        return lax.ppermute(x, ("z", "core"), ring)

    send, keep, send_near, keep_near, own = share(
        channel_count, level_map, s_real, s_imag, prefactor.T, maxwell)
    others = [lax.ppermute(x, "core", swap) for x in send]
    send_near, others[0] = lax.optimization_barrier((send_near, others[0]))
    mine = []
    for block in range(len(send)):
        carry = move(keep[block] + others[block])
        near = keep_near[block] + lax.ppermute(send_near[block], "core", swap)
        carry = move(jnp.concatenate([near[:half] + carry[:half], near[half:chans],
                                      near[chans:chans + half] + carry[half:], near[chans + half:]]))
        mine.append(carry + own[block])
    others = [lax.ppermute(x, "core", swap) for x in mine]
    picks, columns = choose(channel_count, level_map, levels)
    part = spread(0, size, picks, columns, mine[0], others[0])
    part = spread(1, size, picks, columns, mine[1], others[1], part)
    part = lax.all_to_all(part, ("y", "x"), 0, 0, tiled=True).sum(0)
    part = part.reshape(2, n, -1, levels).transpose(1, 0, 2, 3)
    part = lax.all_to_all(part, "z", 0, 0, tiled=True)
    part = part[:, 0] + jnp.roll(part[:, 1], 4, axis=0)
    return jnp.transpose(part, (1, 0, 2))


def solution(mesh):
    fine = Mesh(mesh.devices.reshape(4, 4, 8, 2), ("y", "x", "z", "core"))
    jgrp, energy = ("y", "x"), ("z", "core")
    in_specs = (
        P(jgrp, energy, None, None),
        P(jgrp, energy, None, None),
        P(jgrp, None),
        P(jgrp),
        P(None, energy),
        P(None, energy),
    )
    out_specs = P(("y", "x", "z", "core"), None, None)
    return jax.shard_map(body, mesh=fine, in_specs=in_specs, out_specs=out_specs, check_vma=False)
```

```python
import functools

import jax
import jax.numpy as jnp
from jax import lax
from jax.experimental import pallas as pl
from jax.experimental.pallas import tpu as pltpu
from jax.sharding import Mesh, PartitionSpec as P

PLAN = (((0, 4), (4, 16)), ((0, 16),))
GROUP = 16
LANES = 128


def split2(x):
    hi = x.astype(jnp.bfloat16)
    lo = (x - hi.astype(jnp.float32)).astype(jnp.bfloat16)
    return hi, lo


def split3(x):
    hi, mid = split2(x)
    lo = (x - hi.astype(jnp.float32) - mid.astype(jnp.float32)).astype(jnp.bfloat16)
    return hi, mid, lo


def iota(shape, axis):
    return lax.broadcasted_iota(jnp.int32, shape, axis)


def across(x, lanes):
    return jnp.concatenate([x] * (lanes // LANES), axis=1)


def order(z, core):
    sign = 1 - 2 * core
    return [z + sign, z + sign + 4, z - sign, z - sign + 4, z, z + 4, z + 2 * sign, z - 2 * sign]


def mix(rows_ref, scale_ref, weight, at):
    energies, _, chans = rows_ref.shape
    part = rows_ref[:, at, :].reshape(energies * GROUP, chans)
    temps = weight.shape[0] // GROUP
    hi, lo = split2(weight * jnp.concatenate([scale_ref[at, :]] * temps, axis=0))
    both = jnp.dot(jnp.concatenate([hi, lo], axis=0), part, preferred_element_type=jnp.float32)
    return (both[:temps * GROUP] + both[temps * GROUP:]).reshape(temps, GROUP, chans)


def groups(chans, core):
    half = chans // 2
    for mine in (False, True):
        base = (core if mine else 1 - core) * half
        for low in range(0, half, GROUP):
            at = pl.ds(pl.multiple_of(base + low, GROUP), GROUP)
            yield (low, half + low, at) if mine else (half + low, low, at)


def spread_lanes(energies):
    shape = (3 * energies, energies * GROUP)
    hit = iota(shape, 1) // GROUP == iota(shape, 0) % energies
    return jnp.where(hit, 1.0, 0.0).astype(jnp.bfloat16)


def leaders(block, count_ref, level_ref):
    chans = level_ref.shape[1]
    seg_row = jnp.where(iota((1, chans), 1) < count_ref[block], level_ref[pl.ds(block, 1), :], -1)
    seg_row = seg_row.astype(jnp.float32)
    seg_col = jnp.transpose(jnp.broadcast_to(seg_row, (LANES, chans)))
    same = across(seg_col, chans) == seg_row
    earlier = same & (iota((chans, chans), 1) < iota((chans, chans), 0))
    taken = jnp.dot(jnp.where(earlier, 1.0, 0.0).astype(jnp.bfloat16),
                    jnp.ones((chans, LANES), jnp.bfloat16), preferred_element_type=jnp.float32)
    lead = across(jnp.where((taken == 0.0) & (seg_col >= 0.0), 1.0, 0.0), chans)
    return seg_col, jnp.where(same, lead, 0.0).astype(jnp.bfloat16)


def scales(seg_col, pre_ref):
    energies, levels = pre_ref.shape
    picks = across(seg_col, levels) == iota((seg_col.shape[0], levels), 1).astype(jnp.float32)
    picks = jnp.where(picks, 1.0, 0.0).astype(jnp.bfloat16)
    own = lax.dot_general(picks, jnp.concatenate(split3(pre_ref[...]), axis=0), (((1,), (1,)), ((), ())),
                          preferred_element_type=jnp.float32)
    return jnp.dot(own.astype(jnp.bfloat16), spread_lanes(energies), preferred_element_type=jnp.float32)


def rowsums(block, blocks, energies, real_ref, imag_ref, same_ref, rows_ref):
    chans = same_ref.shape[0]
    jgrp = lax.axis_index("y") * lax.axis_size("x") + lax.axis_index("x")
    factor = (2 * (jgrp * blocks + block) + 1).astype(jnp.float32)
    delta = jnp.where(iota((LANES, LANES), 0) == iota((LANES, LANES), 1), 1.0, 0.0)
    for e in energies:
        real = real_ref[e].astype(jnp.float32)
        imag = imag_ref[e].astype(jnp.float32)
        on = [delta - real[k:k + LANES, k:k + LANES] for k in range(0, chans, LANES)]
        real = jnp.concatenate([
            jnp.concatenate([on[0], real[:LANES, LANES:]], axis=1),
            jnp.concatenate([real[LANES:, :LANES], on[1]], axis=1)], axis=0)
        weighted = ((real ** 2 + imag ** 2) * factor).astype(jnp.bfloat16)
        rowsum = jnp.dot(same_ref[...], weighted, preferred_element_type=jnp.float32)
        rows_ref[e] = rowsum.astype(jnp.bfloat16)


def share_kernel(count_hbm, level_hbm, real_hbm, imag_hbm, pre_hbm, max_hbm, *refs):
    blocks, chans = level_hbm.shape
    outs, refs = refs[:8 * blocks], refs[8 * blocks:]
    (real_ref, imag_ref, count_ref, level_ref, pre_ref, max_ref,
     rows_ref, same_ref, scale_ref, weight_ref, wide_ref, part_sem, small_sem) = refs
    temps, energies = max_ref.shape
    half = chans // 2
    width = energies * GROUP
    core = lax.axis_index("core")
    smalls = []
    for i, pair in enumerate(((count_hbm, count_ref), (level_hbm, level_ref),
                              (pre_hbm, pre_ref), (max_hbm, max_ref))):
        smalls.append(pltpu.make_async_copy(*pair, small_sem.at[i]))
        smalls[-1].start()
    parts = [[] for _ in range(blocks)]
    for block in range(blocks):
        for step, (low, high) in enumerate(PLAN[block]):
            at = pl.ds(low, high - low)
            parts[block].append([
                pltpu.make_async_copy(x_hbm.at[block, at], x_ref.at[block, at], part_sem.at[i, block, step])
                for i, (x_hbm, x_ref) in enumerate(((real_hbm, real_ref), (imag_hbm, imag_ref)))
            ])
            for copy in parts[block][step]:
                copy.start()
    for copy in smalls[:2]:
        copy.wait()
    seg_cols = []
    for block in range(blocks):
        seg_col, same_ref[block] = leaders(block, count_ref, level_ref)
        seg_cols.append(seg_col)
    for block in range(blocks):
        for (low, high), copies in zip(PLAN[block], parts[block]):
            for copy in copies:
                copy.wait()
            rowsums(block, blocks, range(low, high), real_ref.at[block], imag_ref.at[block],
                    same_ref.at[block], rows_ref.at[block])
        if block == 0:
            for copy in smalls[2:]:
                copy.wait()
            wide_ref[...] = jnp.dot(jnp.concatenate(split3(max_ref[...]), axis=1), spread_lanes(energies),
                                    preferred_element_type=jnp.float32)
            hit = iota((GROUP, width), 1) % GROUP == iota((GROUP, width), 0)
            for s, t in enumerate(order(lax.axis_index("z"), core)):
                t = lax.rem(t + temps, temps)
                weight_ref[s * GROUP:(s + 1) * GROUP, :] = jnp.where(hit, wide_ref[pl.ds(t, 1), :], 0.0)
    for block in range(blocks):
        scale_ref[block] = scales(seg_cols[block], pre_ref)
        (send_ref, keep_ref, send_front, keep_front, own_front,
         send_back, keep_back, own_back) = outs[block::blocks]
        for front, _, at in groups(chans, core):
            total = mix(rows_ref.at[block], scale_ref.at[block], weight_ref[...], at)
            low, mine = front % half, front < half
            for k in range(2):
                row = k * half + low
                (keep_ref if mine else send_ref)[row:row + GROUP, :] = total[6 + k if mine else 7 - k]
                if mine:
                    keep_front[row:row + GROUP, :] = total[k]
                    send_back[row:row + GROUP, :] = total[2 + k]
                    own_front[row:row + GROUP, :] = total[4 + k]
                else:
                    keep_back[row:row + GROUP, :] = total[k]
                    send_front[row:row + GROUP, :] = total[2 + k]
                    own_back[row:row + GROUP, :] = total[4 + k]


def choose_kernel(count_ref, level_ref, picks_ref, columns_ref):
    blocks, chans = level_ref.shape
    half = chans // 2
    core = lax.axis_index("core")
    levels = columns_ref.shape[1]
    row = iota((levels // 2, chans), 0)
    wanted = row // 2 * 4 + core * 2 + row % 2
    for block in range(blocks):
        seg = jnp.where(iota((1, chans), 1) < count_ref[block], level_ref[pl.ds(block, 1), :], -1)
        columns_ref[block] = jnp.where(iota((levels, chans), 0) == seg, 1.0, 0.0).astype(jnp.bfloat16)
        turned = jnp.concatenate([seg[:, half:], seg[:, :half]], axis=1)
        seg = jnp.where(core == 0, seg, turned)
        picks_ref[block] = jnp.where(wanted == seg, 1.0, 0.0).astype(jnp.bfloat16)


def float_of(*shape):
    return jax.ShapeDtypeStruct(shape, jnp.float32)


def half_of(*shape):
    return jax.ShapeDtypeStruct(shape, jnp.bfloat16)


def share(counts, level_map, s_real, s_imag, prefactor, maxwell):
    blocks, energies, chans = s_real.shape[:3]
    temps = maxwell.shape[0]
    width = energies * GROUP
    args = (counts, level_map, s_real, s_imag, prefactor, maxwell)
    out = pl.pallas_call(
        share_kernel,
        out_shape=[float_of(chans, chans)] * (8 * blocks),
        in_specs=[pl.BlockSpec(memory_space=pltpu.HBM)] * 6,
        out_specs=[pl.BlockSpec(memory_space=pltpu.VMEM)] * (8 * blocks),
        scratch_shapes=[
            pltpu.VMEM(s_real.shape, jnp.bfloat16),
            pltpu.VMEM(s_imag.shape, jnp.bfloat16),
            pltpu.SMEM(counts.shape, jnp.int32),
            pltpu.VMEM(level_map.shape, jnp.int32),
            pltpu.VMEM(prefactor.shape, jnp.float32),
            pltpu.VMEM(maxwell.shape, jnp.float32),
            pltpu.VMEM(s_real.shape, jnp.bfloat16),
            pltpu.VMEM((blocks, chans, chans), jnp.bfloat16),
            pltpu.VMEM((blocks, chans, width), jnp.float32),
            pltpu.VMEM((temps * GROUP, width), jnp.float32),
            pltpu.VMEM((temps, width), jnp.float32),
            pltpu.SemaphoreType.DMA((2, blocks, 2)),
            pltpu.SemaphoreType.DMA((4,)),
        ],
        compiler_params=pltpu.CompilerParams(vmem_limit_bytes=24 * 2**20),
        name="share",
    )(*[pltpu.with_memory_space_constraint(x, pltpu.HBM) for x in args])
    return [out[i * blocks:(i + 1) * blocks] for i in range(8)]


def choose(counts, level_map, levels):
    blocks, chans = level_map.shape
    return pl.pallas_call(
        choose_kernel,
        out_shape=[half_of(blocks, levels // 2, chans), half_of(blocks, levels, chans)],
        in_specs=[pl.BlockSpec(memory_space=pltpu.SMEM), pl.BlockSpec(memory_space=pltpu.VMEM)],
        out_specs=[pl.BlockSpec(memory_space=pltpu.VMEM)] * 2,
        compiler_params=pltpu.CompilerParams(vmem_limit_bytes=16 * 2**20),
        name="choose",
    )(counts, level_map)


def spread_kernel(block, picks_ref, columns_ref, front_ref, back_ref, other_front, other_back, *refs):
    out_ref = refs[-1]
    size, share = out_ref.shape[0], out_ref.shape[1] // 2
    chans = columns_ref.shape[2]
    half = chans // 2
    for k in range(2):
        at = slice(k * half, (k + 1) * half)
        both = jnp.concatenate([front_ref[at, :] + other_back[at, :],
                                back_ref[at, :] + other_front[at, :]], axis=0)
        hi, lo = split2(both)
        wide = lax.dot_general(jnp.concatenate([hi, lo], axis=0), columns_ref[block], (((1,), (1,)), ((), ())),
                               preferred_element_type=jnp.float32)
        hi, lo = split2(wide[:chans] + wide[chans:])
        term = jnp.dot(picks_ref[block], hi, preferred_element_type=jnp.float32)
        term += jnp.dot(picks_ref[block], lo, preferred_element_type=jnp.float32)
        term = term.reshape(size, share, -1)
        at = slice(k * share, (k + 1) * share)
        out_ref[:, at, :] = term if len(refs) == 1 else refs[0][:, at, :] + term


def spread(block, size, picks, columns, *parts):
    whole = pl.BlockSpec(memory_space=pltpu.VMEM)
    rows, levels = picks.shape[1], columns.shape[1]
    return pl.pallas_call(
        functools.partial(spread_kernel, block),
        out_shape=float_of(size, 2 * rows // size, levels),
        in_specs=[whole] * (2 + len(parts)),
        out_specs=whole,
        compiler_params=pltpu.CompilerParams(vmem_limit_bytes=16 * 2**20),
        name="spread",
    )(picks, columns, *parts)


def body(s_real, s_imag, level_map, channel_count, prefactor, maxwell):
    levels = prefactor.shape[0]
    n = lax.axis_size("z")
    size = lax.axis_size("y") * lax.axis_size("x")
    swap = [(0, 1), (1, 0)]
    ring = [(2 * i, (i + 1) % n * 2) for i in range(n)]
    ring += [(2 * i + 1, (i - 1) % n * 2 + 1) for i in range(n)]

    def move(x):
        return lax.ppermute(x, ("z", "core"), ring)

    send, keep, send_front, keep_front, own_front, send_back, keep_back, own_back = share(
        channel_count, level_map, s_real, s_imag, prefactor.T, maxwell)
    others = [lax.ppermute(x, "core", swap) for x in send]
    (send_front, send_back), others[0] = lax.optimization_barrier(((send_front, send_back), others[0]))
    carries = [move(x + y) for x, y in zip(keep, others)]
    backs = [move(x + lax.ppermute(y, "core", swap)) + z for x, y, z in zip(keep_back, send_back, own_back)]
    fronts = []
    for block, carry in enumerate(carries):
        near = keep_front[block] + lax.ppermute(send_front[block], "core", swap)
        fronts.append(move(near + carry))
    picks, columns = choose(channel_count, level_map, levels)
    part = None
    for block, (front, back) in enumerate(zip(fronts, backs)):
        if part is not None:
            front, part = lax.optimization_barrier((front, part))
        front = front + own_front[block]
        both = front, back, lax.ppermute(front, "core", swap), lax.ppermute(back, "core", swap)
        part = spread(block, size, picks, columns, *both, *(() if part is None else (part,)))
    part = lax.all_to_all(part, ("y", "x"), 0, 0, tiled=True).sum(0)
    part = part.reshape(2, n, -1, levels).transpose(1, 0, 2, 3)
    part = lax.all_to_all(part, "z", 0, 0, tiled=True)
    part = part[:, 0] + jnp.roll(part[:, 1], 4, axis=0)
    return jnp.transpose(part, (1, 0, 2))


def solution(mesh):
    fine = Mesh(mesh.devices.reshape(4, 4, 8, 2), ("y", "x", "z", "core"))
    jgrp, energy = ("y", "x"), ("z", "core")
    in_specs = (
        P(jgrp, energy, None, None),
        P(jgrp, energy, None, None),
        P(jgrp, None),
        P(jgrp),
        P(None, energy),
        P(None, energy),
    )
    out_specs = P(("y", "x", "z", "core"), None, None)
    return jax.shard_map(body, mesh=fine, in_specs=in_specs, out_specs=out_specs, check_vma=False)
```

```python
import functools

import jax
import jax.numpy as jnp
from jax import lax
from jax.experimental import pallas as pl
from jax.experimental.pallas import tpu as pltpu
from jax.sharding import Mesh, PartitionSpec as P

PLAN = (((0, 4), (4, 16)), ((0, 16),))
GROUP = 16
LANES = 128


def split2(x):
    hi = x.astype(jnp.bfloat16)
    lo = (x - hi.astype(jnp.float32)).astype(jnp.bfloat16)
    return hi, lo


def split3(x):
    hi, mid = split2(x)
    lo = (x - hi.astype(jnp.float32) - mid.astype(jnp.float32)).astype(jnp.bfloat16)
    return hi, mid, lo


def iota(shape, axis):
    return lax.broadcasted_iota(jnp.int32, shape, axis)


def across(x, lanes):
    return jnp.concatenate([x] * (lanes // LANES), axis=1)


def order(z, core):
    sign = 1 - 2 * core
    return [z + sign, z + sign + 4, z - sign, z - sign + 4, z, z + 4, z + 2 * sign, z - 2 * sign]


def mix(rows_ref, scale_ref, weight, at):
    energies, _, chans = rows_ref.shape
    part = rows_ref[:, at, :].reshape(energies * GROUP, chans)
    temps = weight.shape[0] // GROUP
    hi, lo = split2(weight * jnp.concatenate([scale_ref[at, :]] * temps, axis=0))
    both = jnp.dot(jnp.concatenate([hi, lo], axis=0), part, preferred_element_type=jnp.float32)
    return (both[:temps * GROUP] + both[temps * GROUP:]).reshape(temps, GROUP, chans)


def groups(chans, core):
    half = chans // 2
    for mine in (False, True):
        base = (core if mine else 1 - core) * half
        for low in range(0, half, GROUP):
            at = pl.ds(pl.multiple_of(base + low, GROUP), GROUP)
            yield (low, half + low, at) if mine else (half + low, low, at)


def spread_lanes(energies):
    shape = (3 * energies, energies * GROUP)
    hit = iota(shape, 1) // GROUP == iota(shape, 0) % energies
    return jnp.where(hit, 1.0, 0.0).astype(jnp.bfloat16)


def leaders(block, count_ref, level_ref):
    chans = level_ref.shape[1]
    seg_row = jnp.where(iota((1, chans), 1) < count_ref[block], level_ref[pl.ds(block, 1), :], -1)
    seg_row = seg_row.astype(jnp.float32)
    seg_col = jnp.transpose(jnp.broadcast_to(seg_row, (LANES, chans)))
    same = across(seg_col, chans) == seg_row
    earlier = same & (iota((chans, chans), 1) < iota((chans, chans), 0))
    taken = jnp.dot(jnp.where(earlier, 1.0, 0.0).astype(jnp.bfloat16),
                    jnp.ones((chans, LANES), jnp.bfloat16), preferred_element_type=jnp.float32)
    lead = across(jnp.where((taken == 0.0) & (seg_col >= 0.0), 1.0, 0.0), chans)
    return seg_col, jnp.where(same, lead, 0.0).astype(jnp.bfloat16)


def scales(seg_col, pre_ref):
    energies, levels = pre_ref.shape
    picks = across(seg_col, levels) == iota((seg_col.shape[0], levels), 1).astype(jnp.float32)
    picks = jnp.where(picks, 1.0, 0.0).astype(jnp.bfloat16)
    own = lax.dot_general(picks, jnp.concatenate(split3(pre_ref[...]), axis=0), (((1,), (1,)), ((), ())),
                          preferred_element_type=jnp.float32)
    return jnp.dot(own.astype(jnp.bfloat16), spread_lanes(energies), preferred_element_type=jnp.float32)


def rowsums(block, blocks, energies, real_ref, imag_ref, same_ref, rows_ref):
    chans = same_ref.shape[0]
    jgrp = lax.axis_index("y") * lax.axis_size("x") + lax.axis_index("x")
    factor = (2 * (jgrp * blocks + block) + 1).astype(jnp.float32)
    delta = jnp.where(iota((LANES, LANES), 0) == iota((LANES, LANES), 1), 1.0, 0.0)
    for e in energies:
        real = real_ref[e].astype(jnp.float32)
        imag = imag_ref[e].astype(jnp.float32)
        on = [delta - real[k:k + LANES, k:k + LANES] for k in range(0, chans, LANES)]
        real = jnp.concatenate([
            jnp.concatenate([on[0], real[:LANES, LANES:]], axis=1),
            jnp.concatenate([real[LANES:, :LANES], on[1]], axis=1)], axis=0)
        weighted = ((real ** 2 + imag ** 2) * factor).astype(jnp.bfloat16)
        rowsum = jnp.dot(same_ref[...], weighted, preferred_element_type=jnp.float32)
        rows_ref[e] = rowsum.astype(jnp.bfloat16)


def share_kernel(count_hbm, level_hbm, real_hbm, imag_hbm, pre_hbm, max_hbm, *refs):
    blocks, chans = level_hbm.shape
    outs, refs = refs[:8 * blocks], refs[8 * blocks:]
    (real_ref, imag_ref, count_ref, level_ref, pre_ref, max_ref,
     rows_ref, same_ref, scale_ref, weight_ref, wide_ref, part_sem, small_sem) = refs
    temps, energies = max_ref.shape
    half = chans // 2
    width = energies * GROUP
    core = lax.axis_index("core")
    smalls = []
    for i, pair in enumerate(((count_hbm, count_ref), (level_hbm, level_ref),
                              (pre_hbm, pre_ref), (max_hbm, max_ref))):
        smalls.append(pltpu.make_async_copy(*pair, small_sem.at[i]))
        smalls[-1].start()
    parts = [[] for _ in range(blocks)]
    for block in range(blocks):
        for step, (low, high) in enumerate(PLAN[block]):
            at = pl.ds(low, high - low)
            parts[block].append([
                pltpu.make_async_copy(x_hbm.at[block, at], x_ref.at[block, at], part_sem.at[i, block, step])
                for i, (x_hbm, x_ref) in enumerate(((real_hbm, real_ref), (imag_hbm, imag_ref)))
            ])
            for copy in parts[block][step]:
                copy.start()
    for copy in smalls[:2]:
        copy.wait()
    seg_cols = []
    for block in range(blocks):
        seg_col, same_ref[block] = leaders(block, count_ref, level_ref)
        seg_cols.append(seg_col)
    for block in range(blocks):
        for (low, high), copies in zip(PLAN[block], parts[block]):
            for copy in copies:
                copy.wait()
            rowsums(block, blocks, range(low, high), real_ref.at[block], imag_ref.at[block],
                    same_ref.at[block], rows_ref.at[block])
        if block == 0:
            for copy in smalls[2:]:
                copy.wait()
            wide_ref[...] = jnp.dot(jnp.concatenate(split3(max_ref[...]), axis=1), spread_lanes(energies),
                                    preferred_element_type=jnp.float32)
            hit = iota((GROUP, width), 1) % GROUP == iota((GROUP, width), 0)
            for s, t in enumerate(order(lax.axis_index("z"), core)):
                t = lax.rem(t + temps, temps)
                weight_ref[s * GROUP:(s + 1) * GROUP, :] = jnp.where(hit, wide_ref[pl.ds(t, 1), :], 0.0)
    for block in range(blocks):
        scale_ref[block] = scales(seg_cols[block], pre_ref)
        (send_ref, keep_ref, send_front, keep_front, own_front,
         send_back, keep_back, own_back) = outs[block::blocks]
        for front, _, at in groups(chans, core):
            total = mix(rows_ref.at[block], scale_ref.at[block], weight_ref[...], at)
            low, mine = front % half, front < half
            for k in range(2):
                row = k * half + low
                (keep_ref if mine else send_ref)[row:row + GROUP, :] = total[6 + k if mine else 7 - k]
                if mine:
                    keep_front[row:row + GROUP, :] = total[k]
                    send_back[row:row + GROUP, :] = total[2 + k]
                    own_front[row:row + GROUP, :] = total[4 + k]
                else:
                    keep_back[row:row + GROUP, :] = total[k]
                    send_front[row:row + GROUP, :] = total[2 + k]
                    own_back[row:row + GROUP, :] = total[4 + k]


def choose_kernel(count_ref, level_ref, picks_ref, columns_ref):
    blocks, chans = level_ref.shape
    half = chans // 2
    core = lax.axis_index("core")
    levels = columns_ref.shape[1]
    row = iota((levels // 2, chans), 0)
    wanted = row // 2 * 4 + core * 2 + row % 2
    for block in range(blocks):
        seg = jnp.where(iota((1, chans), 1) < count_ref[block], level_ref[pl.ds(block, 1), :], -1)
        columns_ref[block] = jnp.where(iota((levels, chans), 0) == seg, 1.0, 0.0).astype(jnp.bfloat16)
        turned = jnp.concatenate([seg[:, half:], seg[:, :half]], axis=1)
        seg = jnp.where(core == 0, seg, turned)
        picks_ref[block] = jnp.where(wanted == seg, 1.0, 0.0).astype(jnp.bfloat16)


def float_of(*shape):
    return jax.ShapeDtypeStruct(shape, jnp.float32)


def half_of(*shape):
    return jax.ShapeDtypeStruct(shape, jnp.bfloat16)


def share(counts, level_map, s_real, s_imag, prefactor, maxwell):
    blocks, energies, chans = s_real.shape[:3]
    temps = maxwell.shape[0]
    width = energies * GROUP
    args = (counts, level_map, s_real, s_imag, prefactor, maxwell)
    out = pl.pallas_call(
        share_kernel,
        out_shape=[float_of(chans, chans)] * (8 * blocks),
        in_specs=[pl.BlockSpec(memory_space=pltpu.HBM)] * 6,
        out_specs=[pl.BlockSpec(memory_space=pltpu.VMEM)] * (8 * blocks),
        scratch_shapes=[
            pltpu.VMEM(s_real.shape, jnp.bfloat16),
            pltpu.VMEM(s_imag.shape, jnp.bfloat16),
            pltpu.SMEM(counts.shape, jnp.int32),
            pltpu.VMEM(level_map.shape, jnp.int32),
            pltpu.VMEM(prefactor.shape, jnp.float32),
            pltpu.VMEM(maxwell.shape, jnp.float32),
            pltpu.VMEM(s_real.shape, jnp.bfloat16),
            pltpu.VMEM((blocks, chans, chans), jnp.bfloat16),
            pltpu.VMEM((blocks, chans, width), jnp.float32),
            pltpu.VMEM((temps * GROUP, width), jnp.float32),
            pltpu.VMEM((temps, width), jnp.float32),
            pltpu.SemaphoreType.DMA((2, blocks, 2)),
            pltpu.SemaphoreType.DMA((4,)),
        ],
        compiler_params=pltpu.CompilerParams(vmem_limit_bytes=24 * 2**20),
        name="share",
    )(*[pltpu.with_memory_space_constraint(x, pltpu.HBM) for x in args])
    return [out[i * blocks:(i + 1) * blocks] for i in range(8)]


def choose(counts, level_map, levels):
    blocks, chans = level_map.shape
    return pl.pallas_call(
        choose_kernel,
        out_shape=[half_of(blocks, levels // 2, chans), half_of(blocks, levels, chans)],
        in_specs=[pl.BlockSpec(memory_space=pltpu.SMEM), pl.BlockSpec(memory_space=pltpu.VMEM)],
        out_specs=[pl.BlockSpec(memory_space=pltpu.VMEM)] * 2,
        compiler_params=pltpu.CompilerParams(vmem_limit_bytes=16 * 2**20),
        name="choose",
    )(counts, level_map)


def spread_kernel(block, picks_ref, columns_ref, front_ref, back_ref, other_front, other_back, *refs):
    out_ref = refs[-1]
    size, share = out_ref.shape[0], out_ref.shape[1] // 2
    chans = columns_ref.shape[2]
    half = chans // 2
    for k in range(2):
        at = slice(k * half, (k + 1) * half)
        both = jnp.concatenate([front_ref[at, :] + other_back[at, :],
                                back_ref[at, :] + other_front[at, :]], axis=0)
        hi, lo = split2(both)
        wide = lax.dot_general(jnp.concatenate([hi, lo], axis=0), columns_ref[block], (((1,), (1,)), ((), ())),
                               preferred_element_type=jnp.float32)
        hi, lo = split2(wide[:chans] + wide[chans:])
        term = jnp.dot(picks_ref[block], hi, preferred_element_type=jnp.float32)
        term += jnp.dot(picks_ref[block], lo, preferred_element_type=jnp.float32)
        term = term.reshape(size, share, -1)
        at = slice(k * share, (k + 1) * share)
        out_ref[:, at, :] = term if len(refs) == 1 else refs[0][:, at, :] + term


def spread(block, size, picks, columns, *parts):
    whole = pl.BlockSpec(memory_space=pltpu.VMEM)
    rows, levels = picks.shape[1], columns.shape[1]
    return pl.pallas_call(
        functools.partial(spread_kernel, block),
        out_shape=float_of(size, 2 * rows // size, levels),
        in_specs=[whole] * (2 + len(parts)),
        out_specs=whole,
        compiler_params=pltpu.CompilerParams(vmem_limit_bytes=16 * 2**20),
        name="spread",
    )(picks, columns, *parts)


def body(s_real, s_imag, level_map, channel_count, prefactor, maxwell):
    levels = prefactor.shape[0]
    n = lax.axis_size("z")
    size = lax.axis_size("y") * lax.axis_size("x")
    swap = [(0, 1), (1, 0)]
    ring = [(2 * i, (i + 1) % n * 2) for i in range(n)]
    ring += [(2 * i + 1, (i - 1) % n * 2 + 1) for i in range(n)]

    def move(x):
        return lax.ppermute(x, ("z", "core"), ring)

    send, keep, send_front, keep_front, own_front, send_back, keep_back, own_back = share(
        channel_count, level_map, s_real, s_imag, prefactor.T, maxwell)
    others = [lax.ppermute(x, "core", swap) for x in send]
    (send_front, send_back), others[0] = lax.optimization_barrier(((send_front, send_back), others[0]))
    carries = [move(x + y) for x, y in zip(keep, others)]
    chosen = choose(channel_count, level_map, levels)
    carries[0], (picks, columns) = lax.optimization_barrier((carries[0], tuple(chosen)))
    backs = [move(x + lax.ppermute(y, "core", swap)) + z for x, y, z in zip(keep_back, send_back, own_back)]
    fronts = []
    for block, carry in enumerate(carries):
        near = keep_front[block] + lax.ppermute(send_front[block], "core", swap)
        fronts.append(move(near + carry) + own_front[block])
    other_backs = [lax.ppermute(x, "core", swap) for x in backs]
    other_fronts = [lax.ppermute(x, "core", swap) for x in fronts]
    part = None
    for block, blocks in enumerate(zip(fronts, backs, other_fronts, other_backs)):
        part = spread(block, size, picks, columns, *blocks, *(() if part is None else (part,)))
    part = lax.all_to_all(part, ("y", "x"), 0, 0, tiled=True).sum(0)
    part = part.reshape(2, n, -1, levels).transpose(1, 0, 2, 3)
    part = lax.all_to_all(part, "z", 0, 0, tiled=True)
    part = part[:, 0] + jnp.roll(part[:, 1], 4, axis=0)
    return jnp.transpose(part, (1, 0, 2))


def solution(mesh):
    fine = Mesh(mesh.devices.reshape(4, 4, 8, 2), ("y", "x", "z", "core"))
    jgrp, energy = ("y", "x"), ("z", "core")
    in_specs = (
        P(jgrp, energy, None, None),
        P(jgrp, energy, None, None),
        P(jgrp, None),
        P(jgrp),
        P(None, energy),
        P(None, energy),
    )
    out_specs = P(("y", "x", "z", "core"), None, None)
    return jax.shard_map(body, mesh=fine, in_specs=in_specs, out_specs=out_specs, check_vma=False)
```

```python
import functools

import jax
import jax.numpy as jnp
from jax import lax
from jax.experimental import pallas as pl
from jax.experimental.pallas import tpu as pltpu
from jax.sharding import Mesh, PartitionSpec as P

PLAN = (((0, 4), (4, 16)), ((0, 16),))
GROUP = 16
LANES = 128


def split2(x):
    hi = x.astype(jnp.bfloat16)
    lo = (x - hi.astype(jnp.float32)).astype(jnp.bfloat16)
    return hi, lo


def split3(x):
    hi, mid = split2(x)
    lo = (x - hi.astype(jnp.float32) - mid.astype(jnp.float32)).astype(jnp.bfloat16)
    return hi, mid, lo


def iota(shape, axis):
    return lax.broadcasted_iota(jnp.int32, shape, axis)


def across(x, lanes):
    return jnp.concatenate([x] * (lanes // LANES), axis=1)


def order(z, core):
    sign = 1 - 2 * core
    return [z + sign, z + sign + 4, z - sign, z - sign + 4, z, z + 4, z + 2 * sign, z - 2 * sign]


def mix(rows_ref, scale_ref, weight, at):
    energies, _, chans = rows_ref.shape
    part = rows_ref[:, at, :].reshape(energies * GROUP, chans)
    temps = weight.shape[0] // GROUP
    hi, lo = split2(weight * jnp.concatenate([scale_ref[at, :]] * temps, axis=0))
    both = jnp.dot(jnp.concatenate([hi, lo], axis=0), part, preferred_element_type=jnp.float32)
    return (both[:temps * GROUP] + both[temps * GROUP:]).reshape(temps, GROUP, chans)


def groups(chans, core):
    half = chans // 2
    for mine in (False, True):
        base = (core if mine else 1 - core) * half
        for low in range(0, half, GROUP):
            at = pl.ds(pl.multiple_of(base + low, GROUP), GROUP)
            yield (low, half + low, at) if mine else (half + low, low, at)


def spread_lanes(energies):
    shape = (3 * energies, energies * GROUP)
    hit = iota(shape, 1) // GROUP == iota(shape, 0) % energies
    return jnp.where(hit, 1.0, 0.0).astype(jnp.bfloat16)


def leaders(block, count_ref, level_ref):
    chans = level_ref.shape[1]
    seg_row = jnp.where(iota((1, chans), 1) < count_ref[block], level_ref[pl.ds(block, 1), :], -1)
    seg_row = seg_row.astype(jnp.float32)
    seg_col = jnp.transpose(jnp.broadcast_to(seg_row, (LANES, chans)))
    same = across(seg_col, chans) == seg_row
    earlier = same & (iota((chans, chans), 1) < iota((chans, chans), 0))
    taken = jnp.dot(jnp.where(earlier, 1.0, 0.0).astype(jnp.bfloat16),
                    jnp.ones((chans, LANES), jnp.bfloat16), preferred_element_type=jnp.float32)
    lead = across(jnp.where((taken == 0.0) & (seg_col >= 0.0), 1.0, 0.0), chans)
    return seg_col, jnp.where(same, lead, 0.0).astype(jnp.bfloat16)


def scales(seg_col, pre_ref):
    energies, levels = pre_ref.shape
    picks = across(seg_col, levels) == iota((seg_col.shape[0], levels), 1).astype(jnp.float32)
    picks = jnp.where(picks, 1.0, 0.0).astype(jnp.bfloat16)
    own = lax.dot_general(picks, jnp.concatenate(split3(pre_ref[...]), axis=0), (((1,), (1,)), ((), ())),
                          preferred_element_type=jnp.float32)
    return jnp.dot(own.astype(jnp.bfloat16), spread_lanes(energies), preferred_element_type=jnp.float32)


def rowsums(block, blocks, energies, real_ref, imag_ref, same_ref, rows_ref):
    chans = same_ref.shape[0]
    jgrp = lax.axis_index("y") * lax.axis_size("x") + lax.axis_index("x")
    factor = (2 * (jgrp * blocks + block) + 1).astype(jnp.float32)
    delta = jnp.where(iota((LANES, LANES), 0) == iota((LANES, LANES), 1), 1.0, 0.0)
    for e in energies:
        real = real_ref[e].astype(jnp.float32)
        imag = imag_ref[e].astype(jnp.float32)
        on = [delta - real[k:k + LANES, k:k + LANES] for k in range(0, chans, LANES)]
        real = jnp.concatenate([
            jnp.concatenate([on[0], real[:LANES, LANES:]], axis=1),
            jnp.concatenate([real[LANES:, :LANES], on[1]], axis=1)], axis=0)
        weighted = ((real ** 2 + imag ** 2) * factor).astype(jnp.bfloat16)
        rowsum = jnp.dot(same_ref[...], weighted, preferred_element_type=jnp.float32)
        rows_ref[e] = rowsum.astype(jnp.bfloat16)


def share_kernel(count_hbm, level_hbm, real_hbm, imag_hbm, pre_hbm, max_hbm, *refs):
    blocks, chans = level_hbm.shape
    outs, refs = refs[:5 * blocks], refs[5 * blocks:]
    (real_ref, imag_ref, count_ref, level_ref, pre_ref, max_ref,
     rows_ref, same_ref, scale_ref, weight_ref, wide_ref, part_sem, small_sem) = refs
    temps, energies = max_ref.shape
    half = chans // 2
    width = energies * GROUP
    core = lax.axis_index("core")
    smalls = []
    for i, pair in enumerate(((count_hbm, count_ref), (level_hbm, level_ref),
                              (pre_hbm, pre_ref), (max_hbm, max_ref))):
        smalls.append(pltpu.make_async_copy(*pair, small_sem.at[i]))
        smalls[-1].start()
    parts = [[] for _ in range(blocks)]
    for block in range(blocks):
        for step, (low, high) in enumerate(PLAN[block]):
            at = pl.ds(low, high - low)
            parts[block].append([
                pltpu.make_async_copy(x_hbm.at[block, at], x_ref.at[block, at], part_sem.at[i, block, step])
                for i, (x_hbm, x_ref) in enumerate(((real_hbm, real_ref), (imag_hbm, imag_ref)))
            ])
            for copy in parts[block][step]:
                copy.start()
    for copy in smalls[:2]:
        copy.wait()
    seg_cols = []
    for block in range(blocks):
        seg_col, same_ref[block] = leaders(block, count_ref, level_ref)
        seg_cols.append(seg_col)
    for block in range(blocks):
        for (low, high), copies in zip(PLAN[block], parts[block]):
            for copy in copies:
                copy.wait()
            rowsums(block, blocks, range(low, high), real_ref.at[block], imag_ref.at[block],
                    same_ref.at[block], rows_ref.at[block])
        if block == 0:
            for copy in smalls[2:]:
                copy.wait()
            wide_ref[...] = jnp.dot(jnp.concatenate(split3(max_ref[...]), axis=1), spread_lanes(energies),
                                    preferred_element_type=jnp.float32)
            hit = iota((GROUP, width), 1) % GROUP == iota((GROUP, width), 0)
            for s, t in enumerate(order(lax.axis_index("z"), core)):
                t = lax.rem(t + temps, temps)
                weight_ref[s * GROUP:(s + 1) * GROUP, :] = jnp.where(hit, wide_ref[pl.ds(t, 1), :], 0.0)
    for block in range(blocks):
        scale_ref[block] = scales(seg_cols[block], pre_ref)
        send_ref, keep_ref, send_near, keep_near, own_ref = outs[block::blocks]
        for front, back, at in groups(chans, core):
            total = mix(rows_ref.at[block], scale_ref.at[block], weight_ref[...], at)
            low, mine = front % half, front < half
            for k in range(2):
                keep_near[k * chans + front:k * chans + front + GROUP, :] = total[k]
                send_near[k * chans + back:k * chans + back + GROUP, :] = total[2 + k]
                own_ref[k * chans + front:k * chans + front + GROUP, :] = total[4 + k]
                first_ref = keep_ref if mine else send_ref
                first_ref[k * half + low:k * half + low + GROUP, :] = total[6 + k if mine else 7 - k]


def choose_kernel(count_ref, level_ref, picks_ref, columns_ref):
    blocks, chans = level_ref.shape
    half = chans // 2
    core = lax.axis_index("core")
    levels = columns_ref.shape[1]
    row = iota((levels // 2, chans), 0)
    wanted = row // 2 * 4 + core * 2 + row % 2
    for block in range(blocks):
        seg = jnp.where(iota((1, chans), 1) < count_ref[block], level_ref[pl.ds(block, 1), :], -1)
        columns_ref[block] = jnp.where(iota((levels, chans), 0) == seg, 1.0, 0.0).astype(jnp.bfloat16)
        turned = jnp.concatenate([seg[:, half:], seg[:, :half]], axis=1)
        seg = jnp.where(core == 0, seg, turned)
        picks_ref[block] = jnp.where(wanted == seg, 1.0, 0.0).astype(jnp.bfloat16)


def float_of(*shape):
    return jax.ShapeDtypeStruct(shape, jnp.float32)


def half_of(*shape):
    return jax.ShapeDtypeStruct(shape, jnp.bfloat16)


def share(counts, level_map, s_real, s_imag, prefactor, maxwell):
    blocks, energies, chans = s_real.shape[:3]
    temps = maxwell.shape[0]
    width = energies * GROUP
    args = (counts, level_map, s_real, s_imag, prefactor, maxwell)
    out = pl.pallas_call(
        share_kernel,
        out_shape=[float_of(chans, chans)] * (2 * blocks) + [float_of(2 * chans, chans)] * (3 * blocks),
        in_specs=[pl.BlockSpec(memory_space=pltpu.HBM)] * 6,
        out_specs=[pl.BlockSpec(memory_space=pltpu.VMEM)] * (5 * blocks),
        scratch_shapes=[
            pltpu.VMEM(s_real.shape, jnp.bfloat16),
            pltpu.VMEM(s_imag.shape, jnp.bfloat16),
            pltpu.SMEM(counts.shape, jnp.int32),
            pltpu.VMEM(level_map.shape, jnp.int32),
            pltpu.VMEM(prefactor.shape, jnp.float32),
            pltpu.VMEM(maxwell.shape, jnp.float32),
            pltpu.VMEM(s_real.shape, jnp.bfloat16),
            pltpu.VMEM((blocks, chans, chans), jnp.bfloat16),
            pltpu.VMEM((blocks, chans, width), jnp.float32),
            pltpu.VMEM((temps * GROUP, width), jnp.float32),
            pltpu.VMEM((temps, width), jnp.float32),
            pltpu.SemaphoreType.DMA((2, blocks, 2)),
            pltpu.SemaphoreType.DMA((4,)),
        ],
        compiler_params=pltpu.CompilerParams(vmem_limit_bytes=24 * 2**20),
        name="share",
    )(*[pltpu.with_memory_space_constraint(x, pltpu.HBM) for x in args])
    return [out[i * blocks:(i + 1) * blocks] for i in range(5)]


def choose(counts, level_map, levels):
    blocks, chans = level_map.shape
    return pl.pallas_call(
        choose_kernel,
        out_shape=[half_of(blocks, levels // 2, chans), half_of(blocks, levels, chans)],
        in_specs=[pl.BlockSpec(memory_space=pltpu.SMEM), pl.BlockSpec(memory_space=pltpu.VMEM)],
        out_specs=[pl.BlockSpec(memory_space=pltpu.VMEM)] * 2,
        compiler_params=pltpu.CompilerParams(vmem_limit_bytes=16 * 2**20),
        name="choose",
    )(counts, level_map)


def spread_kernel(block, picks_ref, columns_ref, mine_ref, other_ref, *refs):
    out_ref = refs[-1]
    size, share = out_ref.shape[0], out_ref.shape[1] // 2
    chans = columns_ref.shape[2]
    half = chans // 2
    for k in range(2):
        low = k * chans
        both = mine_ref[low:low + chans] + jnp.concatenate(
            [other_ref[low + half:low + chans], other_ref[low:low + half]], axis=0)
        hi, lo = split2(both)
        wide = lax.dot_general(jnp.concatenate([hi, lo], axis=0), columns_ref[block], (((1,), (1,)), ((), ())),
                               preferred_element_type=jnp.float32)
        hi, lo = split2(wide[:chans] + wide[chans:])
        term = jnp.dot(picks_ref[block], hi, preferred_element_type=jnp.float32)
        term += jnp.dot(picks_ref[block], lo, preferred_element_type=jnp.float32)
        term = term.reshape(size, share, -1)
        at = slice(k * share, (k + 1) * share)
        out_ref[:, at, :] = term if len(refs) == 1 else refs[0][:, at, :] + term


def spread(block, size, picks, columns, *parts):
    whole = pl.BlockSpec(memory_space=pltpu.VMEM)
    rows, levels = picks.shape[1], columns.shape[1]
    return pl.pallas_call(
        functools.partial(spread_kernel, block),
        out_shape=float_of(size, 2 * rows // size, levels),
        in_specs=[whole] * (2 + len(parts)),
        out_specs=whole,
        compiler_params=pltpu.CompilerParams(vmem_limit_bytes=16 * 2**20),
        name="spread",
    )(picks, columns, *parts)


def body(s_real, s_imag, level_map, channel_count, prefactor, maxwell):
    chans, levels = s_real.shape[2], prefactor.shape[0]
    half = chans // 2
    n = lax.axis_size("z")
    size = lax.axis_size("y") * lax.axis_size("x")
    swap = [(0, 1), (1, 0)]
    ring = [(2 * i, (i + 1) % n * 2) for i in range(n)]
    ring += [(2 * i + 1, (i - 1) % n * 2 + 1) for i in range(n)]

    def move(x):
        return lax.ppermute(x, ("z", "core"), ring)

    send, keep, send_near, keep_near, own = share(
        channel_count, level_map, s_real, s_imag, prefactor.T, maxwell)
    others = [lax.ppermute(x, "core", swap) for x in send]
    send_near, others[0] = lax.optimization_barrier((send_near, others[0]))
    picks, columns = choose(channel_count, level_map, levels)
    mine = []
    for block in range(len(send)):
        carry = move(keep[block] + others[block])
        near = keep_near[block] + lax.ppermute(send_near[block], "core", swap)
        carry = move(jnp.concatenate([near[:half] + carry[:half], near[half:chans],
                                      near[chans:chans + half] + carry[half:], near[chans + half:]]))
        if block == 0:
            carry, picks, columns = lax.optimization_barrier((carry, picks, columns))
        mine.append(carry + own[block])
    others = [lax.ppermute(x, "core", swap) for x in mine]
    part = spread(0, size, picks, columns, mine[0], others[0])
    part = spread(1, size, picks, columns, mine[1], others[1], part)
    part = lax.all_to_all(part, ("y", "x"), 0, 0, tiled=True).sum(0)
    part = part.reshape(2, n, -1, levels).transpose(1, 0, 2, 3)
    part = lax.all_to_all(part, "z", 0, 0, tiled=True)
    part = part[:, 0] + jnp.roll(part[:, 1], 4, axis=0)
    return jnp.transpose(part, (1, 0, 2))


def solution(mesh):
    fine = Mesh(mesh.devices.reshape(4, 4, 8, 2), ("y", "x", "z", "core"))
    jgrp, energy = ("y", "x"), ("z", "core")
    in_specs = (
        P(jgrp, energy, None, None),
        P(jgrp, energy, None, None),
        P(jgrp, None),
        P(jgrp),
        P(None, energy),
        P(None, energy),
    )
    out_specs = P(("y", "x", "z", "core"), None, None)
    return jax.shard_map(body, mesh=fine, in_specs=in_specs, out_specs=out_specs, check_vma=False)
```
